512 devices in a mesh: expert: 64 (over x, z, core), tensor: 8 (over y).
Axes of the slice: x: 4, y: 8, z: 8, core: 2. Of those that a mesh axis runs over, the one named last changes fastest.
Arguments:
- tokens: bfloat16 [8192, 2048], P('expert', 'tensor'), may hold values from -6 to 6
- cotangent: bfloat16 [8192, 2048], P('expert', 'tensor'), may hold values from -6 to 6
- route_ids: int32 [8192, 6], P('expert'), may hold values from 0 to 63, all different within a row
- route_weights: float32 [8192, 6], P('expert'), may hold values from 0.05 to 0.5
- shared_gate: bfloat16 [1408, 2048], P('tensor'), may hold values from -0.125 to 0.125
- shared_up: bfloat16 [1408, 2048], P('tensor'), may hold values from -0.125 to 0.125
- shared_down: bfloat16 [1408, 2048], P('tensor'), may hold values from -0.15625 to 0.15625
- expert_gate: bfloat16 [64, 1408, 2048], P('expert', 'tensor'), may hold values from -0.125 to 0.125
- expert_up: bfloat16 [64, 1408, 2048], P('expert', 'tensor'), may hold values from -0.125 to 0.125
- expert_down: bfloat16 [64, 1408, 2048], P('expert', 'tensor'), may hold values from -0.15625 to 0.15625
Outputs:
- layer_output: bfloat16 [8192, 2048], P('expert', 'tensor')
- input_grad: bfloat16 [8192, 2048], P('expert', 'tensor')
The draws below stay inside these ranges and needn't reach their ends.
Inputs may be any that keep to these rules, and one draw needn't show every extreme that they name: `route_ids`: each row names 6 different experts.
All inputs are finite; a program needn't handle non-finite values.
Results may differ from the reference program's by a relative error of at most 0.0051.
Values may be sent and summed in bfloat16 or wider, within the bound.
A program may use at most 64 MiB of HBM per device.

```python
import math
import jax
import jax.numpy as jnp
from jax import lax

D = 2048
FF = 1408
SF = 1408
TOP = 6
TOK_DEV = 128
EXPERTS = 64
CAP = 6
TOKENS = 8192
N_EXPERT = 64
N_TENSOR = 8


def level_of(rng, dims, pieces, smallest, high):
    level = 1.0
    for dim, blocks in pieces:
        heights = jax.random.uniform(jax.random.fold_in(jax.random.fold_in(rng, 6), dim), (blocks,), jnp.float32, smallest / len(pieces), high / len(pieces))
        level = level * jnp.repeat(jnp.exp(heights), dims[dim] // blocks).reshape((-1,) + (1,) * (len(dims) - 1 - dim))
    return level


def different_ones(stream_key, rows, number_of, top, lift):
    ranking = jax.random.permutation(jax.random.fold_in(stream_key, 1), number_of)
    boost = ranking
    for power in range(3):
        boost = boost * boost // number_of
    boost = boost * lift // number_of
    chance = jax.random.randint(jax.random.fold_in(stream_key, 2), (rows, number_of), 0, 4096) + boost
    fixed_rows = jax.random.permutation(jax.random.fold_in(stream_key, 3), rows)[jnp.arange(number_of) % rows]
    chance = jnp.where(jnp.arange(rows)[:, None] == fixed_rows[None, :], 1 << 14, chance)
    merit = chance * number_of + jnp.arange(number_of)
    return lax.top_k(merit.astype(jnp.int32), top)[1].astype(jnp.int32)


def scatter_about(own_key, extent, scale, most, pieces=(), held_as=jnp.bfloat16):
    array = scale * jax.random.normal(own_key, extent, jnp.float32)
    if pieces:
        array = array * level_of(own_key, extent, pieces, -0.22, 0.18)
    return jnp.clip(array, -most, most).astype(held_as)


def setup_inputs(seed: int = 0) -> dict:
    arg_keys = jax.random.split(jax.random.key(seed), 11)
    return {
        "tokens": scatter_about(arg_keys[0], (TOKENS, D), 1.0, 6.0, ((0, 64), (1, 8))),
        "cotangent": scatter_about(arg_keys[1], (TOKENS, D), 1.0, 6.0, ((0, 64), (1, 8))),
        "route_ids": different_ones(arg_keys[2], TOKENS, EXPERTS, TOP, 1536),
        "route_weights": jnp.clip(jnp.exp(math.log(0.5) - 2.3025851 * jax.random.uniform(arg_keys[3], (TOKENS, TOP), jnp.float32) ** level_of(arg_keys[3], (TOKENS, TOP), ((0, 64),), -0.2, 0.2)), 0.05, 0.5),
        "shared_gate": scatter_about(arg_keys[4], (SF, D), D ** -0.5, 0.125, ((0, 8),)),
        "shared_up": scatter_about(arg_keys[5], (SF, D), D ** -0.5, 0.125, ((0, 8),)),
        "shared_down": scatter_about(arg_keys[6], (SF, D), SF ** -0.5, 0.15625, ((0, 8),)),
        "expert_gate": scatter_about(arg_keys[7], (EXPERTS, FF, D), D ** -0.5, 0.125, ((0, 64), (1, 8))),
        "expert_up": scatter_about(arg_keys[8], (EXPERTS, FF, D), D ** -0.5, 0.125, ((0, 64), (1, 8))),
        "expert_down": scatter_about(arg_keys[9], (EXPERTS, FF, D), FF ** -0.5, 0.15625, ((0, 64), (1, 8))),
    }


def silu_parts(pre_act):
    sigmoid_value = jax.nn.sigmoid(pre_act)
    return pre_act * sigmoid_value, sigmoid_value * (1.0 + pre_act * (1.0 - sigmoid_value))


def round_trip(values):
    return lax.optimization_barrier(values.astype(jnp.bfloat16)).astype(jnp.float32)


def reference(tokens, cotangent, route_ids, route_weights, shared_gate, shared_up, shared_down, expert_gate, expert_up, expert_down):
    per_block = TOK_DEV * TOP
    rows_expert = N_EXPERT * CAP
    flat_ids = route_ids.reshape(N_EXPERT, per_block).astype(jnp.int32)
    expert_ids = jnp.arange(EXPERTS, dtype=jnp.int32)
    one_hot = (flat_ids[:, :, None] == expert_ids[None, None, :]).astype(jnp.int32)
    rank_in = jnp.sum((jnp.cumsum(one_hot, axis=1) - one_hot) * one_hot, axis=2).astype(jnp.int32)
    block_ids = jnp.arange(N_EXPERT, dtype=jnp.int32)[:, None]
    flat_pos = block_ids * per_block + jnp.arange(per_block, dtype=jnp.int32)[None, :]
    target = jnp.where(rank_in < CAP, flat_ids * rows_expert + block_ids * CAP + rank_in, EXPERTS * rows_expert).astype(jnp.int32)
    slot_table = jnp.full((EXPERTS * rows_expert,), -1, jnp.int32).at[target.reshape(-1)].set(flat_pos.reshape(-1).astype(jnp.int32), mode="drop")
    slot_table = slot_table.reshape(EXPERTS, rows_expert)
    gate_flat = route_weights.reshape(-1)
    group_width = FF // N_TENSOR

    def expert_step(carried, inputs):
        out_total, grad_total = carried
        positions, w_gate, w_up, w_down = inputs
        valid_row = positions >= 0
        safe_pos = jnp.maximum(positions, 0).astype(jnp.int32)
        token_ids = (safe_pos // TOP).astype(jnp.int32)
        zero_bf = jnp.zeros((), jnp.bfloat16)
        x_rows = jnp.where(valid_row[:, None], tokens[token_ids], zero_bf)
        c_rows = jnp.where(valid_row[:, None], cotangent[token_ids], zero_bf)
        weights = jnp.where(valid_row, gate_flat[safe_pos], jnp.zeros((), jnp.float32)).astype(jnp.float32)
        grad_rows = (weights[:, None] * c_rows.astype(jnp.float32)).astype(jnp.bfloat16)
        gate_pre = jnp.dot(x_rows, w_gate.T, preferred_element_type=jnp.float32)
        up_pre = jnp.dot(x_rows, w_up.T, preferred_element_type=jnp.float32)
        act_value, act_slope = silu_parts(gate_pre)
        hidden = (act_value * up_pre).astype(jnp.bfloat16)
        grad_hidden = jnp.dot(grad_rows, w_down.T, preferred_element_type=jnp.float32)
        grad_gate = (grad_hidden * up_pre * act_slope).astype(jnp.bfloat16)
        grad_up = (grad_hidden * act_value).astype(jnp.bfloat16)
        value_sum = jnp.zeros((rows_expert, D), jnp.float32)
        input_sum = jnp.zeros((rows_expert, D), jnp.float32)
        for group_index in range(N_TENSOR):
            low_col = group_index * group_width
            high_col = low_col + group_width
            value_sum = value_sum + round_trip(jnp.dot(hidden[:, low_col:high_col], w_down[low_col:high_col], preferred_element_type=jnp.float32))
            input_term = jnp.dot(grad_gate[:, low_col:high_col], w_gate[low_col:high_col], preferred_element_type=jnp.float32)
            input_term = input_term + jnp.dot(grad_up[:, low_col:high_col], w_up[low_col:high_col], preferred_element_type=jnp.float32)
            input_sum = input_sum + round_trip(input_term)
        dest_row = jnp.where(valid_row, token_ids, TOKENS).astype(jnp.int32)
        out_total = out_total.at[dest_row].add(weights[:, None] * value_sum, mode="drop")
        grad_total = grad_total.at[dest_row].add(input_sum, mode="drop")
        return (out_total, grad_total), None

    initial = (jnp.zeros((TOKENS, D), jnp.float32), jnp.zeros((TOKENS, D), jnp.float32))
    (routed_out, routed_grad), unused = lax.scan(expert_step, initial, (slot_table, expert_gate, expert_up, expert_down))

    shared_gate_pre = jnp.dot(tokens, shared_gate.T, preferred_element_type=jnp.float32)
    shared_up_pre = jnp.dot(tokens, shared_up.T, preferred_element_type=jnp.float32)
    shared_act, shared_slope = silu_parts(shared_gate_pre)
    shared_hidden = (shared_act * shared_up_pre).astype(jnp.bfloat16)
    shared_value = jnp.dot(shared_hidden, shared_down, preferred_element_type=jnp.float32)
    shared_grad_hidden = jnp.dot(cotangent, shared_down.T, preferred_element_type=jnp.float32)
    shared_grad_gate = (shared_grad_hidden * shared_up_pre * shared_slope).astype(jnp.bfloat16)
    shared_grad_up = (shared_grad_hidden * shared_act).astype(jnp.bfloat16)
    shared_input = jnp.dot(shared_grad_gate, shared_gate, preferred_element_type=jnp.float32)
    shared_input = shared_input + jnp.dot(shared_grad_up, shared_up, preferred_element_type=jnp.float32)
    return ((shared_value + routed_out).astype(jnp.bfloat16), (shared_input + routed_grad).astype(jnp.bfloat16))
```

```python
import functools

import jax
import jax.numpy as jnp
from jax import lax
from jax.experimental import pallas as pl
from jax.experimental.pallas import tpu as pltpu
from jax.sharding import PartitionSpec as P

MESH = pl.DeviceIdType.MESH
F32 = jnp.float32
BF16 = jnp.bfloat16
CAP = 6
Z_SIZE = 8
OWN_ROWS = tuple(range(6))
SIB_ROWS = tuple(range(6))
NB = 16


def nt_dot(a, b):
    return lax.dot_general(a, b, (((1,), (1,)), ((), ())), preferred_element_type=F32)


def nn_dot(a, b):
    return jnp.dot(a, b, preferred_element_type=F32)


def silu_parts(v):
    s = jax.nn.sigmoid(v)
    return v * s, s * (1.0 + v * (1.0 - s))


def slot_ranks(shape, first, ranks):
    i = lax.broadcasted_iota(jnp.int32, shape, 1)
    inside = (i >= first) & (i < first + len(ranks))
    return jnp.where(inside, i - first + ranks[0], -1).astype(F32)


def kernel(
    dims,
    tok,
    cot,
    ids,
    wts,
    sg_h,
    su_h,
    sd_h,
    eg_h,
    eu_h,
    ed_h,
    out_v,
    out_i,
    sg,
    su,
    sd,
    eg,
    eu,
    ed,
    meta_out,
    meta_in,
    sib,
    full,
    b_send,
    b_recv,
    b_full,
    r_out,
    r_in,
    t_out,
    t_in,
    ret_send,
    ret_recv,
    fin_out,
    fin_in,
    acc_s,
    acc_b,
    comb,
    w_sem,
    sib_send,
    sib_recv,
    ag_send,
    ag_recv,
    rs_send,
    rs_recv,
    a2a_send,
    a2a_recv,
):
    nq, nx, nz, ny = dims
    t_rows, lanes = tok.shape
    hid = sg.shape[0]
    half = ny // 2
    e_me = lax.axis_index("expert")
    y = lax.axis_index("tensor")
    core = e_me % 2
    q = e_me // 2
    x = q // nz
    z = q % nz
    sibling = (e_me + 1 - 2 * core, y)
    sides = ((e_me, (y + 1) % ny), (e_me, (y + ny - 1) % ny))

    def at_offset(d, sign):
        dx = d // nz
        dz = d % nz
        xx = (x + sign * dx + nx) % nx
        zz = (z + sign * dz + nz) % nz
        return (2 * (xx * nz + zz) + core, y)

    loads = [
        pltpu.make_async_copy(h, v, w_sem.at[k])
        for k, (h, v) in enumerate(
            ((sg_h, sg), (su_h, su), (sd_h, sd), (eg_h, eg), (eu_h, eu), (ed_h, ed))
        )
    ]
    for load in loads:
        load.start()

    barrier = pltpu.get_barrier_semaphore()

    @pl.loop(1, nq)
    def _(d):
        pl.semaphore_signal(barrier, inc=1, device_id=at_offset(d, 1), device_id_type=MESH)

    for dev in (sibling, *sides):
        pl.semaphore_signal(barrier, inc=1, device_id=dev, device_id_type=MESH)

    full[0, y] = tok[...]
    full[1, y] = cot[...]

    lane = lax.broadcasted_iota(jnp.int32, (t_rows, 128), 1)
    d_of = lane % nq
    xx = (x + d_of // nz) % nx
    zz = (z + d_of % nz) % nz
    to_core = jnp.where(lane < nq, core, 1 - core)
    e_of = jnp.where(lane < 2 * nq, 2 * (xx * nz + zz) + to_core, -1)
    named = jnp.zeros((t_rows, 128), F32)
    weight = jnp.zeros((t_rows, 128), F32)
    for k in range(ids.shape[1]):
        hit = ids[:, k : k + 1] == e_of
        named = named + jnp.where(hit, 1.0, 0.0)
        weight = weight + jnp.where(hit, wts[:, k : k + 1], 0.0)
    row = lax.broadcasted_iota(jnp.int32, (t_rows, t_rows), 0)
    col = lax.broadcasted_iota(jnp.int32, (t_rows, t_rows), 1)
    before = jnp.where(col < row, 1.0, 0.0).astype(BF16)
    rank = nn_dot(before, named.astype(BF16))
    rank_t = jnp.where(named > 0.0, rank, 1000.0).T
    weight_t = weight.T
    meta_out[0] = rank_t[nq : 2 * nq]
    meta_out[1] = weight_t[nq : 2 * nq]

    pl.semaphore_wait(barrier, nq + 2)

    def send(src, dst, s_sem, r_sem, dev):
        return pltpu.make_async_remote_copy(
            src_ref=src, dst_ref=dst, send_sem=s_sem, recv_sem=r_sem, device_id=dev, device_id_type=MESH
        )

    to_sib = [
        send(meta_out, meta_in, sib_send.at[0], sib_recv.at[0], sibling),
        send(tok, sib.at[0], sib_send.at[1], sib_recv.at[1], sibling),
        send(cot, sib.at[1], sib_send.at[2], sib_recv.at[2], sibling),
    ]
    for copy in to_sib:
        copy.start()

    def steps_of(kind, way):
        return half if (kind + way) % 2 == 0 else half - 1

    def ag_copy(buf, group, kind, way, s):
        blk = (y + (ny - s if way == 0 else s)) % ny
        at = buf.at[kind, blk]
        return send(at, at, ag_send.at[group, kind, way, s], ag_recv.at[group, kind, way, s], sides[way])

    def ag_block(way, s):
        return (y + (ny - 1 - s if way == 0 else 1 + s)) % ny

    pairs = [(kind, way) for kind in range(2) for way in range(2)]

    def cols(ref, blk):
        return ref[:, pl.ds(pl.multiple_of(blk * lanes, lanes), lanes)]

    def shared_first(kind, blk, first=False):
        v = full[kind, blk]
        for k, w in ((0, sg), (1, su)) if kind == 0 else ((2, sd),):
            term = nt_dot(v, cols(w, blk))
            acc_s[k] = term if first else acc_s[k] + term

    def routed_first(kind, blk, first=False):
        v = b_full[kind, blk]
        for k, w in ((0, eg), (1, eu)) if kind == 0 else ((2, ed),):
            term = nt_dot(v, cols(w, blk))
            acc_b[k] = term if first else acc_b[k] + term

    def gather(buf, group, compute, begun=False):
        for s in range(half):
            for kind, way in pairs:
                if s < steps_of(kind, way) and not (begun and s == 0):
                    if s > 0:
                        ag_copy(buf, group, kind, way, s - 1).wait_recv()
                    ag_copy(buf, group, kind, way, s).start()
            for kind, way in pairs:
                if s == 0:
                    if way == 0:
                        compute(kind, y, True)
                elif s < steps_of(kind, way):
                    compute(kind, ag_block(way, s - 1))
        for kind, way in pairs:
            n = steps_of(kind, way)
            if n < half:
                ag_copy(buf, group, kind, way, n - 1).wait_recv()
                compute(kind, ag_block(way, n - 1))
        for kind, way in pairs:
            n = steps_of(kind, way)
            if n == half:
                ag_copy(buf, group, kind, way, n - 1).wait_recv()
                compute(kind, ag_block(way, n - 1))
        for kind, way in pairs:
            for s in range(steps_of(kind, way)):
                ag_copy(buf, group, kind, way, s).wait_send()

    for kind, way in pairs:
        ag_copy(full, 0, kind, way, 0).start()

    shape = (nq, NB, t_rows)
    own_rank = slot_ranks(shape, 0, OWN_ROWS)
    sib_rank = slot_ranks(shape, len(OWN_ROWS), SIB_ROWS)

    def place(rank_rows, weight_rows, wanted):
        pick = jnp.where(rank_rows.reshape(nq, 1, t_rows) == wanted, 1.0, 0.0)
        scaled = pick * weight_rows.reshape(nq, 1, t_rows)
        return pick.reshape(nq * NB, t_rows), scaled.reshape(nq * NB, t_rows)

    own_pick, own_scaled = place(rank_t[:nq], weight_t[:nq], own_rank)
    for copy in to_sib:
        copy.wait_recv()
    sib_pick, sib_scaled = place(meta_in[0], meta_in[1], sib_rank)
    slot_weight = jnp.sum(own_scaled, axis=1, keepdims=True) + jnp.sum(sib_scaled, axis=1, keepdims=True)
    own_bf, sib_bf = own_pick.astype(BF16), sib_pick.astype(BF16)
    x_rows = nn_dot(own_bf, tok[...]) + nn_dot(sib_bf, sib[0])
    g_rows = slot_weight * (nn_dot(own_bf, cot[...]) + nn_dot(sib_bf, sib[1]))
    slabs = jnp.concatenate((x_rows.reshape(nq, NB, lanes), g_rows.reshape(nq, NB, lanes)), axis=1)
    b_send[...] = slabs.astype(BF16)

    def out_copy(d):
        return send(b_send.at[d], b_recv.at[d], a2a_send.at[0, d], a2a_recv.at[0, d], at_offset(d, 1))

    @pl.loop(1, nq)
    def _(d):
        out_copy(d).start()

    b_recv[0] = b_send[0]

    for k, (pick, scaled) in enumerate(((own_pick, own_scaled), (sib_pick, sib_scaled))):
        high = scaled.astype(BF16).astype(F32)
        comb[k, 0] = pick.T.astype(BF16)
        comb[k, 1] = high.T.astype(BF16)
        comb[k, 2] = (scaled - high).T.astype(BF16)

    for load in loads[:3]:
        load.wait()
    gather(full, 0, shared_first, begun=True)

    @pl.loop(1, nq)
    def _(d):
        out_copy(d).wait_recv()

    arrived = b_recv[...].astype(F32)
    b_full[0, y] = arrived[:, :NB].reshape(nq * NB, lanes).astype(BF16)
    b_full[1, y] = arrived[:, NB:].reshape(nq * NB, lanes).astype(BF16)
    for load in loads[3:]:
        load.wait()
    gather(b_full, 1, routed_first)

    def middle(acc):
        gate, up, grad = acc[0], acc[1], acc[2]
        act, slope = silu_parts(gate)
        return (
            (act * up).astype(BF16),
            (grad * up * slope).astype(BF16),
            (grad * act).astype(BF16),
        )

    hidden_b, gate_b, up_b = middle(acc_b)

    def routed_second(kind, blk):
        if kind == 0:
            return nn_dot(hidden_b, cols(ed, blk))
        return nn_dot(gate_b, cols(eg, blk)) + nn_dot(up_b, cols(eu, blk))

    def rs_target(kind, way, s):
        far = steps_of(kind, way) - s
        return (y + (far if way == 0 else ny - far)) % ny

    def rs_copy(o, i, group, kind, way, s):
        return send(
            o.at[kind, way, s],
            i.at[kind, way, s],
            rs_send.at[group, kind, way, s],
            rs_recv.at[group, kind, way, s],
            sides[way],
        )

    def scatter(o, i, group, compute):
        for s in range(half):
            for kind, way in pairs:
                if s < steps_of(kind, way):
                    term = compute(kind, rs_target(kind, way, s))
                    if s > 0:
                        rs_copy(o, i, group, kind, way, s - 1).wait_recv()
                        term = term + i[kind, way, s - 1].astype(F32)
                    o[kind, way, s] = term.astype(BF16)
                    rs_copy(o, i, group, kind, way, s).start()
        totals = []
        for kind in range(2):
            total = compute(kind, y)
            for way in range(2):
                n = steps_of(kind, way)
                rs_copy(o, i, group, kind, way, n - 1).wait_recv()
                total = total + i[kind, way, n - 1].astype(F32)
            totals.append(total)
        return totals

    def scatter_end(o, i, group):
        for kind, way in pairs:
            for s in range(steps_of(kind, way)):
                rs_copy(o, i, group, kind, way, s).wait_send()

    value_b, input_b = scatter(r_out, r_in, 0, routed_second)
    slabs = jnp.concatenate((value_b.reshape(nq, NB, lanes), input_b.reshape(nq, NB, lanes)), axis=1)
    ret_send[...] = slabs.astype(BF16)

    def back_copy(d):
        return send(ret_send.at[d], ret_recv.at[d], a2a_send.at[1, d], a2a_recv.at[1, d], at_offset(d, -1))

    @pl.loop(1, nq)
    def _(d):
        back_copy(d).start()

    ret_recv[0] = ret_send[0]

    hidden_s, gate_s, up_s = middle(acc_s)

    def shared_second(kind, blk):
        if kind == 0:
            return nn_dot(hidden_s, cols(sd, blk))
        return nn_dot(gate_s, cols(sg, blk)) + nn_dot(up_s, cols(su, blk))

    value_t, input_t = scatter(t_out, t_in, 1, shared_second)

    @pl.loop(1, nq)
    def _(d):
        back_copy(d).wait_recv()

    arrived = ret_recv[...].astype(F32)
    value_r = arrived[:, :NB].reshape(nq * NB, lanes).astype(BF16)
    input_r = arrived[:, NB:].reshape(nq * NB, lanes).astype(BF16)

    fin_out[0] = nn_dot(comb[1, 1], value_r) + nn_dot(comb[1, 2], value_r)
    fin_out[1] = nn_dot(comb[1, 0], input_r)
    last = send(fin_out, fin_in, sib_send.at[3], sib_recv.at[3], sibling)
    last.start()
    value_t = value_t + nn_dot(comb[0, 1], value_r) + nn_dot(comb[0, 2], value_r)
    input_t = input_t + nn_dot(comb[0, 0], input_r)
    last.wait_recv()
    out_v[...] = (value_t + fin_in[0]).astype(BF16)
    out_i[...] = (input_t + fin_in[1]).astype(BF16)

    scatter_end(r_out, r_in, 0)
    scatter_end(t_out, t_in, 1)
    for copy in (*to_sib, last):
        copy.wait_send()

    @pl.loop(1, nq)
    def _(d):
        out_copy(d).wait_send()
        back_copy(d).wait_send()


def on_device(*args):
    tokens, cotangent, route_ids, route_weights, sg, su, sd, eg, eu, ed = args
    ny = lax.axis_size("tensor")
    nq = lax.axis_size("expert") // 2
    nz = min(Z_SIZE, nq)
    t_rows, lanes = tokens.shape
    hid, feats = sg.shape
    half = ny // 2
    eg, eu, ed = (w.reshape(hid, feats) for w in (eg, eu, ed))
    rows = nq * NB
    vmem, dma = pltpu.VMEM, pltpu.SemaphoreType.DMA
    out = jax.ShapeDtypeStruct((t_rows, lanes), BF16)
    in_vmem = pl.BlockSpec(memory_space=pltpu.VMEM)
    in_any = pl.BlockSpec(memory_space=pl.ANY)
    return pl.pallas_call(
        functools.partial(kernel, (nq, nq // nz, nz, ny)),
        out_shape=(out, out),
        in_specs=[in_vmem] * 4 + [in_any] * 6,
        out_specs=(in_vmem, in_vmem),
        scratch_shapes=[
            *[vmem((hid, feats), BF16)] * 6,
            vmem((2, nq, t_rows), F32),
            vmem((2, nq, t_rows), F32),
            vmem((2, t_rows, lanes), BF16),
            vmem((2, ny, t_rows, lanes), BF16),
            vmem((nq, 2 * NB, lanes), BF16),
            vmem((nq, 2 * NB, lanes), BF16),
            vmem((2, ny, rows, lanes), BF16),
            vmem((2, 2, half, rows, lanes), BF16),
            vmem((2, 2, half, rows, lanes), BF16),
            vmem((2, 2, half, t_rows, lanes), BF16),
            vmem((2, 2, half, t_rows, lanes), BF16),
            vmem((nq, 2 * NB, lanes), BF16),
            vmem((nq, 2 * NB, lanes), BF16),
            vmem((2, t_rows, lanes), F32),
            vmem((2, t_rows, lanes), F32),
            vmem((3, t_rows, hid), F32),
            vmem((3, rows, hid), F32),
            vmem((2, 3, t_rows, rows), BF16),
            dma((6,)),
            dma((4,)),
            dma((4,)),
            dma((2, 2, 2, half)),
            dma((2, 2, 2, half)),
            dma((2, 2, 2, half)),
            dma((2, 2, 2, half)),
            dma((2, nq)),
            dma((2, nq)),
        ],
        compiler_params=pltpu.CompilerParams(
            collective_id=0, has_side_effects=True, vmem_limit_bytes=56 * 2**20
        ),
        name="routed_layer",
    )(tokens, cotangent, route_ids, route_weights, sg, su, sd, eg, eu, ed)


def solution(mesh):
    in_specs = (
        P("expert", "tensor"),
        P("expert", "tensor"),
        P("expert", None),
        P("expert", None),
        P("tensor", None),
        P("tensor", None),
        P("tensor", None),
        P("expert", "tensor", None),
        P("expert", "tensor", None),
        P("expert", "tensor", None),
    )
    out_specs = (P("expert", "tensor"), P("expert", "tensor"))
    return jax.shard_map(
        on_device, mesh=mesh, in_specs=in_specs, out_specs=out_specs, check_vma=False
    )
```

```python
import functools

import jax
import jax.numpy as jnp
from jax import lax
from jax.experimental import pallas as pl
from jax.experimental.pallas import tpu as pltpu
from jax.sharding import PartitionSpec as P

MESH = pl.DeviceIdType.MESH
F32 = jnp.float32
BF16 = jnp.bfloat16
CAP = 6
Z_SIZE = 8
WIDE = 4
OWN_ROWS = (4, 5)
SIB_ROWS = (0, 1, 2, 3, 4, 5)
NB = len(OWN_ROWS) + len(SIB_ROWS)
NA = 2 * WIDE
NEAR = 3


def nt_dot(a, b):
    return lax.dot_general(a, b, (((1,), (1,)), ((), ())), preferred_element_type=F32)


def nn_dot(a, b):
    return jnp.dot(a, b, preferred_element_type=F32)


def silu_parts(v):
    s = jax.nn.sigmoid(v)
    return v * s, s * (1.0 + v * (1.0 - s))


def slot_ranks(shape, first, ranks):
    i = lax.broadcasted_iota(jnp.int32, shape, 1)
    inside = (i >= first) & (i < first + len(ranks))
    return jnp.where(inside, i - first + ranks[0], -1).astype(F32)


def kernel(
    dims,
    tok,
    cot,
    ids,
    wts,
    sg_h,
    su_h,
    sd_h,
    eg_h,
    eu_h,
    ed_h,
    out_v,
    out_i,
    sg,
    su,
    sd,
    eg,
    eu,
    ed,
    meta_out,
    meta_in,
    sib,
    full,
    b_send,
    b_recv,
    b_full,
    r_out,
    r_in,
    t_out,
    t_in,
    ret_send,
    ret_recv,
    near_send,
    far_send,
    near_recv,
    far_recv,
    near_back,
    far_back,
    near_home,
    far_home,
    fin_out,
    fin_in,
    acc_s,
    acc_b,
    acc_a,
    comb,
    comb_a,
    w_sem,
    sib_send,
    sib_recv,
    ag_send,
    ag_recv,
    rs_send,
    rs_recv,
    a2a_send,
    a2a_recv,
):
    nq, nx, nz, ny = dims
    t_rows, lanes = tok.shape
    half = ny // 2
    e_me = lax.axis_index("expert")
    y = lax.axis_index("tensor")
    core = e_me % 2
    q = e_me // 2
    x = q // nz
    z = q % nz
    sibling = (e_me + 1 - 2 * core, y)
    sides = ((e_me, (y + 1) % ny), (e_me, (y + ny - 1) % ny))
    pairs = [(kind, way) for kind in range(2) for way in range(2)]
    offsets = [0]
    for s in range(1, half):
        offsets += [-s, s]
    offsets += [half]

    def block_at(off):
        return (y + off + ny) % ny

    def at_offset(d, sign):
        dx = d // nz
        dz = d % nz
        xx = (x + sign * dx + nx) % nx
        zz = (z + sign * dz + nz) % nz
        return (2 * (xx * nz + zz) + core, y)

    def send(src, dst, s_sem, r_sem, dev):
        return pltpu.make_async_remote_copy(
            src_ref=src, dst_ref=dst, send_sem=s_sem, recv_sem=r_sem, device_id=dev, device_id_type=MESH
        )

    def cols(ref, blk):
        return ref[:, pl.ds(pl.multiple_of(blk * lanes, lanes), lanes)]

    loads = [
        pltpu.make_async_copy(h, v, w_sem.at[k])
        for k, (h, v) in enumerate(
            ((sg_h, sg), (su_h, su), (sd_h, sd), (eg_h, eg), (eu_h, eu), (ed_h, ed))
        )
    ]
    for load in loads:
        load.start()

    barrier = pltpu.get_barrier_semaphore()

    @pl.loop(1, nq)
    def _(d):
        pl.semaphore_signal(barrier, inc=1, device_id=at_offset(d, 1), device_id_type=MESH)

    for dev in (sibling, *sides):
        pl.semaphore_signal(barrier, inc=1, device_id=dev, device_id_type=MESH)

    full[0, y] = tok[...]
    full[1, y] = cot[...]

    line = lax.broadcasted_iota(jnp.int32, (2 * nq, t_rows), 0)
    d_of = line % nq
    xx = (x + d_of // nz) % nx
    zz = (z + d_of % nz) % nz
    e_of = 2 * (xx * nz + zz) + jnp.where(line < nq, core, 1 - core)
    named = jnp.zeros((2 * nq, t_rows), F32)
    weight = jnp.zeros((2 * nq, t_rows), F32)
    for k in range(ids.shape[0]):
        hit = ids[k : k + 1, :] == e_of
        named = named + jnp.where(hit, 1.0, 0.0)
        weight = weight + jnp.where(hit, wts[k : k + 1, :], 0.0)
    row = lax.broadcasted_iota(jnp.int32, (t_rows, t_rows), 0)
    col = lax.broadcasted_iota(jnp.int32, (t_rows, t_rows), 1)
    before = jnp.where(row < col, 1.0, 0.0).astype(BF16)
    rank = jnp.where(named > 0.0, nn_dot(named.astype(BF16), before), 1000.0)
    meta_out[0] = rank[nq:]
    meta_out[1] = weight[nq:]

    pl.semaphore_wait(barrier, nq + 2)

    to_sib = [
        send(meta_out, meta_in, sib_send.at[0], sib_recv.at[0], sibling),
        send(tok, sib.at[0], sib_send.at[1], sib_recv.at[1], sibling),
        send(cot, sib.at[1], sib_send.at[2], sib_recv.at[2], sibling),
    ]
    for copy in to_sib:
        copy.start()

    def steps_of(kind, way):
        return half if (kind + way) % 2 == 0 else half - 1

    def ag_copy(buf, group, kind, way, s):
        at = buf.at[kind, block_at(-s if way == 0 else s)]
        return send(at, at, ag_send.at[group, kind, way, s], ag_recv.at[group, kind, way, s], sides[way])

    def ag_start(buf, group):
        for kind, way in pairs:
            ag_copy(buf, group, kind, way, 0).start()

    def ag_step(buf, group, s):
        for kind, way in pairs:
            ag_copy(buf, group, kind, way, s - 1).wait_recv()
            if s < steps_of(kind, way):
                ag_copy(buf, group, kind, way, s).start()

    def ag_last(buf, group):
        for kind, way in pairs:
            if steps_of(kind, way) == half:
                ag_copy(buf, group, kind, way, half - 1).wait_recv()

    def ag_end(buf, group):
        for kind, way in pairs:
            for s in range(steps_of(kind, way)):
                ag_copy(buf, group, kind, way, s).wait_send()

    ag_start(full, 0)

    def first_layer(acc, v, g, weights, blk, first):
        gate, up, down = weights
        for k, (rows, w) in enumerate(((v, gate), (v, up), (g, down))):
            term = nt_dot(rows, cols(w, blk))
            acc[k] = term if first else acc[k] + term

    def shared_first(off):
        blk = block_at(off)
        first_layer(acc_s, full[0, blk], full[1, blk], (sg, su, sd), blk, off == 0)

    def routed_first(off):
        blk = block_at(off)
        first_layer(acc_b, b_full[0, blk], b_full[1, blk], (eg, eu, ed), blk, off == 0)

    shape = (nq, NB, t_rows)
    own_rank = slot_ranks(shape, 0, OWN_ROWS)
    sib_rank = slot_ranks(shape, len(OWN_ROWS), SIB_ROWS)

    def place(rank_rows, weight_rows, wanted):
        n = wanted.shape[1]
        pick = jnp.where(rank_rows.reshape(nq, 1, t_rows) == wanted, 1.0, 0.0)
        scaled = pick * weight_rows.reshape(nq, 1, t_rows)
        return pick.reshape(nq * n, t_rows), scaled.reshape(nq * n, t_rows)

    own_pick, own_scaled = place(rank[:nq], weight[:nq], own_rank)
    for copy in to_sib:
        copy.wait_recv()
    sib_pick, sib_scaled = place(meta_in[0], meta_in[1], sib_rank)
    slot_weight = jnp.sum(own_scaled, axis=1, keepdims=True) + jnp.sum(sib_scaled, axis=1, keepdims=True)
    own_bf, sib_bf = own_pick.astype(BF16), sib_pick.astype(BF16)
    x_rows = nn_dot(own_bf, tok[...]) + nn_dot(sib_bf, sib[0])
    g_rows = slot_weight * (nn_dot(own_bf, cot[...]) + nn_dot(sib_bf, sib[1]))
    slabs = jnp.concatenate((x_rows.reshape(nq, NB, lanes), g_rows.reshape(nq, NB, lanes)), axis=1)
    b_send[...] = slabs.astype(BF16)

    def swap_copy(k, src, dst, sign):
        def at(d):
            return send(src.at[d], dst.at[d], a2a_send.at[k, d], a2a_recv.at[k, d], at_offset(d, sign))

        return at

    def start_all(copy):
        @pl.loop(1, nq)
        def _(d):
            copy(d).start()

    def wait_all(copy):
        @pl.loop(1, nq)
        def _(d):
            copy(d).wait_recv()

    b_out = swap_copy(0, b_send, b_recv, 1)
    near_out = swap_copy(1, near_send, near_recv, 1)
    far_out = swap_copy(2, far_send, far_recv, 1)
    far_in = swap_copy(3, far_back, far_home, -1)
    near_in = swap_copy(4, near_back, near_home, -1)
    b_in = swap_copy(5, ret_send, ret_recv, -1)

    start_all(b_out)
    b_recv[0] = b_send[0]

    slot = lax.broadcasted_iota(jnp.int32, (nq, NA, t_rows), 1)
    wide_rank = jnp.where(slot < WIDE, slot, slot - WIDE).astype(F32)
    wide_pick, wide_scaled = place(rank[:nq], weight[:nq], wide_rank)
    slot = slot.reshape(nq * NA, t_rows)
    top = slot < WIDE
    x_pick = jnp.where(top, wide_pick, 0.0).astype(BF16)
    g_pick = jnp.where(top, 0.0, wide_pick).astype(BF16)
    slot = lax.broadcasted_iota(jnp.int32, (nq, NA, 1), 1).reshape(nq * NA, 1)
    row_scale = jnp.where(slot < WIDE, 1.0, jnp.sum(wide_scaled, axis=1, keepdims=True))

    def wide_rows(p):
        blk = block_at(offsets[p])
        rows = row_scale * (nn_dot(x_pick, full[0, blk]) + nn_dot(g_pick, full[1, blk]))
        rows = rows.reshape(nq, NA, lanes).astype(BF16)
        if p < NEAR:
            near_send[:, :, p * lanes : (p + 1) * lanes] = rows
        else:
            far_send[:, :, (p - NEAR) * lanes : (p - NEAR + 1) * lanes] = rows

    for load in loads[:3]:
        load.wait()
    wide_rows(0)
    shared_first(0)
    for s in range(1, half):
        ag_step(full, 0, s)
        for p in (2 * s - 1, 2 * s):
            wide_rows(p)
        if s == 1:
            start_all(near_out)
            near_recv[0] = near_send[0]
        for p in (2 * s - 1, 2 * s):
            shared_first(offsets[p])
    ag_last(full, 0)

    wait_all(b_out)
    arrived = b_recv[...].astype(F32)
    b_full[0, y] = arrived[:, :NB].reshape(nq * NB, lanes).astype(BF16)
    b_full[1, y] = arrived[:, NB:].reshape(nq * NB, lanes).astype(BF16)
    ag_start(b_full, 1)

    wide_rows(ny - 1)
    start_all(far_out)
    far_recv[0] = far_send[0]
    shared_first(half)

    for k, (pick, scaled) in enumerate(((own_pick, own_scaled), (sib_pick, sib_scaled))):
        high = scaled.astype(BF16).astype(F32)
        comb[k, 0] = pick.T.astype(BF16)
        comb[k, 1] = high.T.astype(BF16)
        comb[k, 2] = (scaled - high).T.astype(BF16)
    wide_scaled = jnp.where(top, wide_scaled, 0.0)
    high = wide_scaled.astype(BF16).astype(F32)
    comb_a[0] = jnp.where(top, 0.0, wide_pick).T.astype(BF16)
    comb_a[1] = high.T.astype(BF16)
    comb_a[2] = (wide_scaled - high).T.astype(BF16)

    def middle(gate, up, grad):
        act, slope = silu_parts(gate)
        return (
            (act * up).astype(BF16),
            (grad * up * slope).astype(BF16),
            (grad * act).astype(BF16),
        )

    def second_layer(mid, weights):
        hidden, grad_gate, grad_up = mid
        gate, up, down = weights

        def of(kind, blk):
            if kind == 0:
                return nn_dot(hidden, cols(down, blk))
            return nn_dot(grad_gate, cols(gate, blk)) + nn_dot(grad_up, cols(up, blk))

        return of

    for load in loads[3:]:
        load.wait()
    routed_first(0)
    for s in range(1, half):
        ag_step(b_full, 1, s)
        routed_first(-s)
        routed_first(s)
    shared_mid = middle(acc_s[0], acc_s[1], acc_s[2])
    ag_last(b_full, 1)
    routed_first(half)
    routed_second = second_layer(middle(acc_b[0], acc_b[1], acc_b[2]), (eg, eu, ed))

    def rs_offset(kind, way, s):
        far = steps_of(kind, way) - s
        return far if way == 0 else -far

    def rs_copy(o, i, group, kind, way, s):
        return send(
            o.at[kind, way, s],
            i.at[kind, way, s],
            rs_send.at[group, kind, way, s],
            rs_recv.at[group, kind, way, s],
            sides[way],
        )

    def rs_step(o, i, group, s, compute):
        for kind, way in pairs:
            if s < steps_of(kind, way):
                term = compute(kind, rs_offset(kind, way, s))
                if s > 0:
                    rs_copy(o, i, group, kind, way, s - 1).wait_recv()
                    term = term + i[kind, way, s - 1].astype(F32)
                o[kind, way, s] = term.astype(BF16)
                rs_copy(o, i, group, kind, way, s).start()

    def rs_total(o, i, group, compute):
        totals = []
        for kind in range(2):
            total = compute(kind, 0)
            for way in range(2):
                n = steps_of(kind, way)
                rs_copy(o, i, group, kind, way, n - 1).wait_recv()
                total = total + i[kind, way, n - 1].astype(F32)
            totals.append(total)
        return totals

    def rs_end(o, i, group):
        for kind, way in pairs:
            for s in range(steps_of(kind, way)):
                rs_copy(o, i, group, kind, way, s).wait_send()

    def routed_term(kind, off):
        return routed_second(kind, block_at(off))

    rs_step(r_out, r_in, 0, 0, routed_term)

    wait_all(near_out)
    for p in range(NEAR):
        blk = block_at(offsets[p])
        v = near_recv[:, :, p * lanes : (p + 1) * lanes].astype(F32).reshape(nq * NA, lanes).astype(BF16)
        first_layer(acc_a, v, v, (eg, eu, ed), blk, p == 0)
    wait_all(far_out)
    for p in range(NEAR, ny):
        blk = block_at(offsets[p])
        v = far_recv[:, :, (p - NEAR) * lanes : (p - NEAR + 1) * lanes]
        v = v.astype(F32).reshape(nq * NA, lanes).astype(BF16)
        first_layer(acc_a, v, v, (eg, eu, ed), blk, False)
    hid = sg.shape[0]
    slot = lax.broadcasted_iota(jnp.int32, (nq, NA, hid), 1).reshape(nq * NA, hid)
    top_hid = slot < WIDE
    gate_a, up_a = acc_a[0], acc_a[1]
    act, slope = silu_parts(gate_a)
    hidden_a = jnp.where(top_hid, act * up_a, 0.0).astype(BF16)

    def lowered(v):
        v = v.reshape(nq, NA, hid)
        return jnp.concatenate((v[:, WIDE:], v[:, :WIDE]), axis=1).reshape(nq * NA, hid)

    grad_a = acc_a[2]
    grad_gate_a = jnp.where(top_hid, 0.0, grad_a * lowered(up_a) * lowered(slope)).astype(BF16)
    grad_up_a = jnp.where(top_hid, 0.0, grad_a * lowered(act)).astype(BF16)
    wide_second = second_layer((hidden_a, grad_gate_a, grad_up_a), (eg, eu, ed))

    def wide_back(p):
        blk = block_at(offsets[p])
        rows = (wide_second(0, blk) + wide_second(1, blk)).reshape(nq, NA, lanes).astype(BF16)
        if p < NEAR:
            near_back[:, :, p * lanes : (p + 1) * lanes] = rows
        else:
            far_back[:, :, (p - NEAR) * lanes : (p - NEAR + 1) * lanes] = rows

    for p in range(NEAR, ny):
        wide_back(p)
    start_all(far_in)
    far_home[0] = far_back[0]
    for p in range(NEAR):
        wide_back(p)
    start_all(near_in)
    near_home[0] = near_back[0]

    for s in range(1, half):
        rs_step(r_out, r_in, 0, s, routed_term)
    value_b, input_b = rs_total(r_out, r_in, 0, routed_term)
    slabs = jnp.concatenate((value_b.reshape(nq, NB, lanes), input_b.reshape(nq, NB, lanes)), axis=1)
    ret_send[...] = slabs.astype(BF16)
    start_all(b_in)
    ret_recv[0] = ret_send[0]

    shared_second = second_layer(shared_mid, (sg, su, sd))

    def token_term(kind, off):
        p = offsets.index(off if -off != half else half)
        home, at = (near_home, p) if p < NEAR else (far_home, p - NEAR)
        rows = home[:, :, at * lanes : (at + 1) * lanes]
        rows = rows.astype(F32).reshape(nq * NA, lanes).astype(BF16)
        total = shared_second(kind, block_at(off))
        if kind == 0:
            return total + nn_dot(comb_a[1], rows) + nn_dot(comb_a[2], rows)
        return total + nn_dot(comb_a[0], rows)

    wait_all(far_in)
    near_from = half - 2
    for s in range(half):
        if s == near_from:
            wait_all(near_in)
        rs_step(t_out, t_in, 1, s, token_term)
    value_t, input_t = rs_total(t_out, t_in, 1, token_term)

    wait_all(b_in)
    arrived = ret_recv[...].astype(F32)
    value_r = arrived[:, :NB].reshape(nq * NB, lanes).astype(BF16)
    input_r = arrived[:, NB:].reshape(nq * NB, lanes).astype(BF16)

    fin_out[0] = nn_dot(comb[1, 1], value_r) + nn_dot(comb[1, 2], value_r)
    fin_out[1] = nn_dot(comb[1, 0], input_r)
    last = send(fin_out, fin_in, sib_send.at[3], sib_recv.at[3], sibling)
    last.start()
    value_t = value_t + nn_dot(comb[0, 1], value_r) + nn_dot(comb[0, 2], value_r)
    input_t = input_t + nn_dot(comb[0, 0], input_r)
    last.wait_recv()
    out_v[...] = (value_t + fin_in[0]).astype(BF16)
    out_i[...] = (input_t + fin_in[1]).astype(BF16)

    ag_end(full, 0)
    ag_end(b_full, 1)
    rs_end(r_out, r_in, 0)
    rs_end(t_out, t_in, 1)
    for copy in (*to_sib, last):
        copy.wait_send()

    @pl.loop(1, nq)
    def _(d):
        for copy in (b_out, near_out, far_out, far_in, near_in, b_in):
            copy(d).wait_send()


def on_device(*args):
    tokens, cotangent, route_ids, route_weights, sg, su, sd, eg, eu, ed = args
    ny = lax.axis_size("tensor")
    nq = lax.axis_size("expert") // 2
    nz = min(Z_SIZE, nq)
    t_rows, lanes = tokens.shape
    hid, feats = sg.shape
    half = ny // 2
    eg, eu, ed = (w.reshape(hid, feats) for w in (eg, eu, ed))
    rows = nq * NB
    vmem, dma = pltpu.VMEM, pltpu.SemaphoreType.DMA
    out = jax.ShapeDtypeStruct((t_rows, lanes), BF16)
    in_vmem = pl.BlockSpec(memory_space=pltpu.VMEM)
    in_any = pl.BlockSpec(memory_space=pl.ANY)
    return pl.pallas_call(
        functools.partial(kernel, (nq, nq // nz, nz, ny)),
        out_shape=(out, out),
        in_specs=[in_vmem] * 4 + [in_any] * 6,
        out_specs=(in_vmem, in_vmem),
        scratch_shapes=[
            *[vmem((hid, feats), BF16)] * 6,
            vmem((2, nq, t_rows), F32),
            vmem((2, nq, t_rows), F32),
            vmem((2, t_rows, lanes), BF16),
            vmem((2, ny, t_rows, lanes), BF16),
            vmem((nq, 2 * NB, lanes), BF16),
            vmem((nq, 2 * NB, lanes), BF16),
            vmem((2, ny, rows, lanes), BF16),
            vmem((2, 2, half, rows, lanes), BF16),
            vmem((2, 2, half, rows, lanes), BF16),
            vmem((2, 2, half, t_rows, lanes), BF16),
            vmem((2, 2, half, t_rows, lanes), BF16),
            vmem((nq, 2 * NB, lanes), BF16),
            vmem((nq, 2 * NB, lanes), BF16),
            *[vmem((nq, NA, n * lanes), BF16) for n in (NEAR, ny - NEAR)] * 4,
            vmem((2, t_rows, lanes), F32),
            vmem((2, t_rows, lanes), F32),
            vmem((3, t_rows, hid), F32),
            vmem((3, rows, hid), F32),
            vmem((3, nq * NA, hid), F32),
            vmem((2, 3, t_rows, rows), BF16),
            vmem((3, t_rows, nq * NA), BF16),
            dma((6,)),
            dma((4,)),
            dma((4,)),
            dma((2, 2, 2, half)),
            dma((2, 2, 2, half)),
            dma((2, 2, 2, half)),
            dma((2, 2, 2, half)),
            dma((6, nq)),
            dma((6, nq)),
        ],
        compiler_params=pltpu.CompilerParams(
            collective_id=0, has_side_effects=True, vmem_limit_bytes=56 * 2**20
        ),
        name="routed_layer",
    )(tokens, cotangent, route_ids.T, route_weights.T, sg, su, sd, eg, eu, ed)


def solution(mesh):
    in_specs = (
        P("expert", "tensor"),
        P("expert", "tensor"),
        P("expert", None),
        P("expert", None),
        P("tensor", None),
        P("tensor", None),
        P("tensor", None),
        P("expert", "tensor", None),
        P("expert", "tensor", None),
        P("expert", "tensor", None),
    )
    out_specs = (P("expert", "tensor"), P("expert", "tensor"))
    return jax.shard_map(
        on_device, mesh=mesh, in_specs=in_specs, out_specs=out_specs, check_vma=False
    )
```

```python
import functools

import jax
import jax.numpy as jnp
from jax import lax
from jax.experimental import pallas as pl
from jax.experimental.pallas import tpu as pltpu
from jax.sharding import PartitionSpec as P

MESH = pl.DeviceIdType.MESH
F32 = jnp.float32
BF16 = jnp.bfloat16
CAP = 6
Z_SIZE = 8
WIDE = 4
OWN_ROWS = (4, 5)
SIB_ROWS = (0, 1, 2, 3, 4, 5)
NB = len(OWN_ROWS) + len(SIB_ROWS)
NA = 2 * WIDE
NEAR = 3


def nt_dot(a, b):
    return lax.dot_general(a, b, (((1,), (1,)), ((), ())), preferred_element_type=F32)


def nn_dot(a, b):
    return jnp.dot(a, b, preferred_element_type=F32)


def silu_parts(v):
    s = jax.nn.sigmoid(v)
    return v * s, s * (1.0 + v * (1.0 - s))


def slot_ranks(shape, first, ranks):
    i = lax.broadcasted_iota(jnp.int32, shape, 1)
    inside = (i >= first) & (i < first + len(ranks))
    return jnp.where(inside, i - first + ranks[0], -1).astype(F32)


def kernel(
    dims,
    tok,
    cot,
    ids,
    wts,
    sg_h,
    su_h,
    sd_h,
    eg_h,
    eu_h,
    ed_h,
    out_v,
    out_i,
    sg,
    su,
    sd,
    eg,
    eu,
    ed,
    meta_out,
    meta_in,
    sib,
    full,
    b_send,
    b_recv,
    b_full,
    r_out,
    r_in,
    t_out,
    t_in,
    ret_send,
    ret_recv,
    near_send,
    far_send,
    near_recv,
    far_recv,
    near_back,
    far_back,
    near_home,
    far_home,
    fin_out,
    fin_in,
    acc_s,
    acc_b,
    acc_a,
    comb,
    comb_a,
    w_sem,
    sib_send,
    sib_recv,
    ag_send,
    ag_recv,
    rs_send,
    rs_recv,
    a2a_send,
    a2a_recv,
    round_sem,
):
    nq, nx, nz, ny = dims
    t_rows, lanes = tok.shape
    half = ny // 2
    e_me = lax.axis_index("expert")
    y = lax.axis_index("tensor")
    core = e_me % 2
    q = e_me // 2
    x = q // nz
    z = q % nz
    sibling = (e_me + 1 - 2 * core, y)
    sides = ((e_me, (y + 1) % ny), (e_me, (y + ny - 1) % ny))
    pairs = [(kind, way) for kind in range(2) for way in range(2)]
    offsets = [0]
    for s in range(1, half):
        offsets += [-s, s]
    offsets += [half]

    def block_at(off):
        return lax.rem(y + off + ny, ny)

    def at_offset(d, sign):
        dx = lax.div(d, nz) if not isinstance(d, int) else d // nz
        dz = lax.rem(d, nz) if not isinstance(d, int) else d % nz
        xx = lax.rem(x + dx if sign > 0 else x - dx + nx, nx)
        zz = lax.rem(z + dz if sign > 0 else z - dz + nz, nz)
        return (2 * (xx * nz + zz) + core, y)

    def send(src, dst, s_sem, r_sem, dev):
        return pltpu.make_async_remote_copy(
            src_ref=src, dst_ref=dst, send_sem=s_sem, recv_sem=r_sem, device_id=dev, device_id_type=MESH
        )

    def cols(ref, blk):
        return ref[:, pl.ds(pl.multiple_of(blk * lanes, lanes), lanes)]

    barrier = pltpu.get_barrier_semaphore()
    column = [at_offset(k * nz, 1) for k in range(1, nx)]
    greeted = [*sides, sibling, *column, *(at_offset(k, 1) for k in range(1, nz))]
    for dev in greeted:
        pl.semaphore_signal(barrier, inc=1, device_id=dev, device_id_type=MESH)

    loads = [
        pltpu.make_async_copy(h, v, w_sem.at[k])
        for k, (h, v) in enumerate(
            ((sg_h, sg), (su_h, su), (sd_h, sd), (eg_h, eg), (eu_h, eu), (ed_h, ed))
        )
    ]
    for load in loads:
        load.start()

    full[0, y] = tok[...]
    full[1, y] = cot[...]

    def steps_of(kind, way):
        return half if (kind + way) % 2 == 0 else half - 1

    def ag_copy(buf, group, kind, way, s):
        at = buf.at[kind, block_at(-s if way == 0 else s)]
        return send(at, at, ag_send.at[group, kind, way, s], ag_recv.at[group, kind, way, s], sides[way])

    def ag_start(buf, group):
        for kind, way in pairs:
            ag_copy(buf, group, kind, way, 0).start()

    def ag_step(buf, group, s):
        for kind, way in pairs:
            ag_copy(buf, group, kind, way, s - 1).wait_recv()
            if s < steps_of(kind, way):
                ag_copy(buf, group, kind, way, s).start()

    def ag_last(buf, group):
        for kind, way in pairs:
            if steps_of(kind, way) == half:
                ag_copy(buf, group, kind, way, half - 1).wait_recv()

    def ag_end(buf, group):
        for kind, way in pairs:
            for s in range(steps_of(kind, way)):
                ag_copy(buf, group, kind, way, s).wait_send()

    pl.semaphore_wait(barrier, len(greeted))
    ag_start(full, 0)
    to_sib = [
        send(tok, sib.at[0], sib_send.at[1], sib_recv.at[1], sibling),
        send(cot, sib.at[1], sib_send.at[2], sib_recv.at[2], sibling),
    ]
    for copy in to_sib:
        copy.start()
    for dev in column:
        pl.semaphore_signal(round_sem, inc=1, device_id=dev, device_id_type=MESH)

    line = lax.broadcasted_iota(jnp.int32, (2 * nq, t_rows), 0)
    d_of = line % nq
    xx = (x + d_of // nz) % nx
    zz = (z + d_of % nz) % nz
    e_of = 2 * (xx * nz + zz) + jnp.where(line < nq, core, 1 - core)
    named = jnp.zeros((2 * nq, t_rows), F32)
    weight = jnp.zeros((2 * nq, t_rows), F32)
    for k in range(ids.shape[0]):
        hit = ids[k : k + 1, :] == e_of
        named = named + jnp.where(hit, 1.0, 0.0)
        weight = weight + jnp.where(hit, wts[k : k + 1, :], 0.0)
    row = lax.broadcasted_iota(jnp.int32, (t_rows, t_rows), 0)
    col = lax.broadcasted_iota(jnp.int32, (t_rows, t_rows), 1)
    before = jnp.where(row < col, 1.0, 0.0).astype(BF16)
    rank = jnp.where(named > 0.0, nn_dot(named.astype(BF16), before), 1000.0)
    meta_out[0] = rank[nq:]
    meta_out[1] = weight[nq:]

    to_sib.append(send(meta_out, meta_in, sib_send.at[0], sib_recv.at[0], sibling))
    to_sib[2].start()

    def first_layer(acc, v, g, weights, blk, first):
        gate, up, down = weights
        for k, (rows, w) in enumerate(((v, gate), (v, up), (g, down))):
            term = nt_dot(rows, cols(w, blk))
            acc[k] = term if first else acc[k] + term

    def shared_first(off):
        blk = block_at(off)
        first_layer(acc_s, full[0, blk], full[1, blk], (sg, su, sd), blk, off == 0)

    def routed_first(h, off):
        blk = block_at(off)
        first_layer(acc_b.at[h], b_full[h, 0, blk], b_full[h, 1, blk], (eg, eu, ed), blk, off == 0)

    shape = (nq, NB, t_rows)
    own_rank = slot_ranks(shape, 0, OWN_ROWS)
    sib_rank = slot_ranks(shape, len(OWN_ROWS), SIB_ROWS)

    def place(rank_rows, weight_rows, wanted):
        n = wanted.shape[1]
        pick = jnp.where(rank_rows.reshape(nq, 1, t_rows) == wanted, 1.0, 0.0)
        scaled = pick * weight_rows.reshape(nq, 1, t_rows)
        return pick.reshape(nq * n, t_rows), scaled.reshape(nq * n, t_rows)

    own_pick, own_scaled = place(rank[:nq], weight[:nq], own_rank)
    ag_step(full, 0, 1)
    for copy in to_sib:
        copy.wait_recv()
    sib_pick, sib_scaled = place(meta_in[0], meta_in[1], sib_rank)
    slot_weight = jnp.sum(own_scaled, axis=1, keepdims=True) + jnp.sum(sib_scaled, axis=1, keepdims=True)
    own_bf, sib_bf = own_pick.astype(BF16), sib_pick.astype(BF16)
    x_rows = nn_dot(own_bf, tok[...]) + nn_dot(sib_bf, sib[0])
    g_rows = slot_weight * (nn_dot(own_bf, cot[...]) + nn_dot(sib_bf, sib[1]))
    slabs = jnp.concatenate((x_rows.reshape(nq, NB, lanes), g_rows.reshape(nq, NB, lanes)), axis=1)
    b_send[...] = slabs.astype(BF16)

    def swap_copy(k, src, dst, sign):
        def at(d):
            return send(src.at[d], dst.at[d], a2a_send.at[k, d], a2a_recv.at[k, d], at_offset(d, sign))

        return at

    def start_all(copy, first=1, last=nq):
        @pl.loop(first, last)
        def _(d):
            copy(d).start()

    def wait_all(copy, first=1, last=nq):
        @pl.loop(first, last)
        def _(d):
            copy(d).wait_recv()

    b_out = swap_copy(0, b_send, b_recv, 1)
    near_out = swap_copy(1, near_send, near_recv, 1)
    far_out = swap_copy(2, far_send, far_recv, 1)
    far_in = swap_copy(3, far_back, far_home, -1)
    near_in = swap_copy(4, near_back, near_home, -1)
    b_in = swap_copy(5, ret_send, ret_recv, -1)

    if nx > 1:
        pl.semaphore_wait(round_sem, nx - 1)
    start_all(b_out)
    b_recv[0] = b_send[0]

    slot = lax.broadcasted_iota(jnp.int32, (nq, NA, t_rows), 1)
    wide_rank = jnp.where(slot < WIDE, slot, slot - WIDE).astype(F32)
    wide_pick, wide_scaled = place(rank[:nq], weight[:nq], wide_rank)
    slot = slot.reshape(nq * NA, t_rows)
    top = slot < WIDE
    x_pick = jnp.where(top, wide_pick, 0.0).astype(BF16)
    g_pick = jnp.where(top, 0.0, wide_pick).astype(BF16)
    slot = lax.broadcasted_iota(jnp.int32, (nq, NA, 1), 1).reshape(nq * NA, 1)
    row_scale = jnp.where(slot < WIDE, 1.0, jnp.sum(wide_scaled, axis=1, keepdims=True))

    def wide_rows(p):
        blk = block_at(offsets[p])
        rows = row_scale * (nn_dot(x_pick, full[0, blk]) + nn_dot(g_pick, full[1, blk]))
        rows = rows.reshape(nq, NA, lanes).astype(BF16)
        if p < NEAR:
            near_send[:, :, p * lanes : (p + 1) * lanes] = rows
        else:
            far_send[:, :, (p - NEAR) * lanes : (p - NEAR + 1) * lanes] = rows

    mid = nq // 2

    def unpack_slabs(ref, h):
        v = ref[h * mid : (h + 1) * mid].astype(F32)
        return [v[:, k * NB : (k + 1) * NB].reshape(mid * NB, lanes) for k in range(2)]

    for p in range(NEAR):
        wide_rows(p)
    start_all(near_out)
    near_recv[0] = near_send[0]
    for s in range(2, half):
        ag_step(full, 0, s)
        for p in (2 * s - 1, 2 * s):
            wide_rows(p)

    for h in range(2):
        wait_all(b_out, max(1, h * mid), (h + 1) * mid)
        for kind, v in enumerate(unpack_slabs(b_recv, h)):
            b_full[h, kind, y] = v.astype(BF16)
        ag_start(b_full.at[h], 1 + h)
    ag_last(full, 0)
    wide_rows(ny - 1)
    start_all(far_out)
    far_recv[0] = far_send[0]

    for k, (pick, scaled) in enumerate(((own_pick, own_scaled), (sib_pick, sib_scaled))):
        high = scaled.astype(BF16).astype(F32)
        comb[k, 0] = pick.T.astype(BF16)
        comb[k, 1] = high.T.astype(BF16)
        comb[k, 2] = (scaled - high).T.astype(BF16)
    wide_scaled = jnp.where(top, wide_scaled, 0.0)
    high = wide_scaled.astype(BF16).astype(F32)
    comb_a[0] = jnp.where(top, 0.0, wide_pick).T.astype(BF16)
    comb_a[1] = high.T.astype(BF16)
    comb_a[2] = (wide_scaled - high).T.astype(BF16)

    def middle(gate, up, grad):
        act, slope = silu_parts(gate)
        return (
            (act * up).astype(BF16),
            (grad * up * slope).astype(BF16),
            (grad * act).astype(BF16),
        )

    def second_layer(mid, weights):
        hidden, grad_gate, grad_up = mid
        gate, up, down = weights

        def of(kind, blk):
            if kind == 0:
                return nn_dot(hidden, cols(down, blk))
            return nn_dot(grad_gate, cols(gate, blk)) + nn_dot(grad_up, cols(up, blk))

        return of

    for load in loads:
        load.wait()
    todo = list(offsets)
    for s in range(1, half):
        for h in range(2):
            ag_step(b_full.at[h], 1 + h, s)
            for off in ([0] if s == 1 else []) + [-s, s]:
                routed_first(h, off)
            share = -(-len(todo) // (2 * (half - s) - h))
            for off in todo[:share]:
                shared_first(off)
            todo = todo[share:]
    shared_mid = middle(acc_s[0], acc_s[1], acc_s[2])

    def take_wide(p):
        ref, at = (near_recv, p) if p < NEAR else (far_recv, p - NEAR)
        v = ref[:, :, at * lanes : (at + 1) * lanes].astype(F32).reshape(nq * NA, lanes).astype(BF16)
        first_layer(acc_a, v, v, (eg, eu, ed), block_at(offsets[p]), p == 0)

    def rs_offset(kind, way, s):
        far = steps_of(kind, way) - s
        return far if way == 0 else -far

    def rs_copy(o, i, group, kind, way, s):
        return send(
            o.at[kind, way, s],
            i.at[kind, way, s],
            rs_send.at[group, kind, way, s],
            rs_recv.at[group, kind, way, s],
            sides[way],
        )

    def rs_step(o, i, group, s, compute):
        for kind, way in pairs:
            if s < steps_of(kind, way):
                term = compute(kind, rs_offset(kind, way, s))
                if s > 0:
                    rs_copy(o, i, group, kind, way, s - 1).wait_recv()
                    term = term + i[kind, way, s - 1].astype(F32)
                o[kind, way, s] = term.astype(BF16)
                rs_copy(o, i, group, kind, way, s).start()

    def rs_total(o, i, group, compute):
        totals = []
        for kind in range(2):
            total = compute(kind, 0)
            for way in range(2):
                n = steps_of(kind, way)
                rs_copy(o, i, group, kind, way, n - 1).wait_recv()
                total = total + i[kind, way, n - 1].astype(F32)
            totals.append(total)
        return totals

    def rs_end(o, i, group):
        for kind, way in pairs:
            for s in range(steps_of(kind, way)):
                rs_copy(o, i, group, kind, way, s).wait_send()

    second_b = []

    def routed_term(h):
        return lambda kind, off: second_b[h](kind, block_at(off))

    def routed_step(h, s):
        rs_step(r_out.at[h], r_in.at[h], 1 + h, s, routed_term(h))

    for h in range(2):
        ag_last(b_full.at[h], 1 + h)
        routed_first(h, half)
        second_b.append(second_layer(middle(acc_b[h, 0], acc_b[h, 1], acc_b[h, 2]), (eg, eu, ed)))
        routed_step(h, 0)

    wait_all(near_out)
    for p in range(NEAR):
        take_wide(p)
    wait_all(far_out)
    for p in range(NEAR, ny):
        take_wide(p)
    routed_step(0, 1)
    hid = sg.shape[0]
    slot = lax.broadcasted_iota(jnp.int32, (nq, NA, hid), 1).reshape(nq * NA, hid)
    top_hid = slot < WIDE
    gate_a, up_a = acc_a[0], acc_a[1]
    act, slope = silu_parts(gate_a)
    hidden_a = jnp.where(top_hid, act * up_a, 0.0).astype(BF16)

    def lowered(v):
        v = v.reshape(nq, NA, hid)
        return jnp.concatenate((v[:, WIDE:], v[:, :WIDE]), axis=1).reshape(nq * NA, hid)

    grad_a = acc_a[2]
    grad_gate_a = jnp.where(top_hid, 0.0, grad_a * lowered(up_a) * lowered(slope)).astype(BF16)
    grad_up_a = jnp.where(top_hid, 0.0, grad_a * lowered(act)).astype(BF16)
    wide_second = second_layer((hidden_a, grad_gate_a, grad_up_a), (eg, eu, ed))

    def wide_back(p):
        blk = block_at(offsets[p])
        rows = (wide_second(0, blk) + wide_second(1, blk)).reshape(nq, NA, lanes).astype(BF16)
        if p < NEAR:
            near_back[:, :, p * lanes : (p + 1) * lanes] = rows
        else:
            far_back[:, :, (p - NEAR) * lanes : (p - NEAR + 1) * lanes] = rows

    for p in range(NEAR, ny):
        wide_back(p)
    start_all(far_in)
    far_home[0] = far_back[0]
    routed_step(1, 1)
    for p in range(NEAR):
        wide_back(p)
    start_all(near_in)
    near_home[0] = near_back[0]
    for s in range(2, half):
        for h in range(2):
            routed_step(h, s)

    shared_second = second_layer(shared_mid, (sg, su, sd))

    def token_term(kind, off):
        p = offsets.index(off if -off != half else half)
        home, at = (near_home, p) if p < NEAR else (far_home, p - NEAR)
        rows = home[:, :, at * lanes : (at + 1) * lanes]
        rows = rows.astype(F32).reshape(nq * NA, lanes).astype(BF16)
        total = shared_second(kind, block_at(off))
        if kind == 0:
            return total + nn_dot(comb_a[1], rows) + nn_dot(comb_a[2], rows)
        return total + nn_dot(comb_a[0], rows)

    def send_home(h):
        pair = rs_total(r_out.at[h], r_in.at[h], 1 + h, routed_term(h))
        slabs = jnp.concatenate([v.reshape(mid, NB, lanes) for v in pair], axis=1)
        ret_send[h * mid : (h + 1) * mid] = slabs.astype(BF16)
        start_all(b_in, max(1, h * mid), (h + 1) * mid)

    send_home(0)
    near_from = half - 2
    wait_all(far_in)
    for s in range(half):
        if s == near_from:
            wait_all(near_in)
        rs_step(t_out, t_in, 0, s, token_term)
        if s == 0:
            send_home(1)
            ret_recv[0] = ret_send[0]

    wait_all(b_in)
    halves = [unpack_slabs(ret_recv, h) for h in range(2)]
    value_r, input_r = (jnp.concatenate([v[k] for v in halves], axis=0).astype(BF16) for k in range(2))

    fin_out[0] = nn_dot(comb[1, 1], value_r) + nn_dot(comb[1, 2], value_r)
    fin_out[1] = nn_dot(comb[1, 0], input_r)
    last = send(fin_out, fin_in, sib_send.at[3], sib_recv.at[3], sibling)
    last.start()
    value_t, input_t = rs_total(t_out, t_in, 0, token_term)
    value_t = value_t + nn_dot(comb[0, 1], value_r) + nn_dot(comb[0, 2], value_r)
    input_t = input_t + nn_dot(comb[0, 0], input_r)
    last.wait_recv()
    out_v[...] = (value_t + fin_in[0]).astype(out_v.dtype)
    out_i[...] = (input_t + fin_in[1]).astype(out_i.dtype)

    ag_end(full, 0)
    rs_end(t_out, t_in, 0)
    for h in range(2):
        ag_end(b_full.at[h], 1 + h)
        rs_end(r_out.at[h], r_in.at[h], 1 + h)
    for copy in (*to_sib, last):
        copy.wait_send()

    @pl.loop(1, nq)
    def _(d):
        for copy in (b_out, near_out, far_out, far_in, near_in, b_in):
            copy(d).wait_send()


def on_device(*args):
    tokens, cotangent, route_ids, route_weights, sg, su, sd, eg, eu, ed = args
    ny = lax.axis_size("tensor")
    nq = lax.axis_size("expert") // 2
    nz = min(Z_SIZE, nq)
    t_rows, lanes = tokens.shape
    hid, feats = sg.shape
    half = ny // 2
    eg, eu, ed = (w.reshape(hid, feats) for w in (eg, eu, ed))
    rows = nq * NB
    vmem, dma = pltpu.VMEM, pltpu.SemaphoreType.DMA
    out = jax.ShapeDtypeStruct((t_rows, lanes), BF16)
    in_vmem = pl.BlockSpec(memory_space=pltpu.VMEM)
    in_any = pl.BlockSpec(memory_space=pl.ANY)
    return pl.pallas_call(
        functools.partial(kernel, (nq, nq // nz, nz, ny)),
        out_shape=(out, out),
        in_specs=[in_vmem] * 4 + [in_any] * 6,
        out_specs=(in_vmem, in_vmem),
        scratch_shapes=[
            *[vmem((hid, feats), BF16)] * 6,
            vmem((2, nq, t_rows), F32),
            vmem((2, nq, t_rows), F32),
            vmem((2, t_rows, lanes), BF16),
            vmem((2, ny, t_rows, lanes), BF16),
            vmem((nq, 2 * NB, lanes), BF16),
            vmem((nq, 2 * NB, lanes), BF16),
            vmem((2, 2, ny, rows // 2, lanes), BF16),
            vmem((2, 2, 2, half, rows // 2, lanes), BF16),
            vmem((2, 2, 2, half, rows // 2, lanes), BF16),
            vmem((2, 2, half, t_rows, lanes), BF16),
            vmem((2, 2, half, t_rows, lanes), BF16),
            vmem((nq, 2 * NB, lanes), BF16),
            vmem((nq, 2 * NB, lanes), BF16),
            *[vmem((nq, NA, n * lanes), BF16) for n in (NEAR, ny - NEAR)] * 4,
            vmem((2, t_rows, lanes), F32),
            vmem((2, t_rows, lanes), F32),
            vmem((3, t_rows, hid), F32),
            vmem((2, 3, rows // 2, hid), F32),
            vmem((3, nq * NA, hid), F32),
            vmem((2, 3, t_rows, rows), BF16),
            vmem((3, t_rows, nq * NA), BF16),
            dma((6,)),
            dma((4,)),
            dma((4,)),
            dma((3, 2, 2, half)),
            dma((3, 2, 2, half)),
            dma((3, 2, 2, half)),
            dma((3, 2, 2, half)),
            dma((6, nq)),
            dma((6, nq)),
            pltpu.SemaphoreType.REGULAR,
        ],
        compiler_params=pltpu.CompilerParams(
            collective_id=0, has_side_effects=True, vmem_limit_bytes=56 * 2**20
        ),
        name="routed_layer",
    )(tokens, cotangent, route_ids.T, route_weights.T, sg, su, sd, eg, eu, ed)


def solution(mesh):
    in_specs = (
        P("expert", "tensor"),
        P("expert", "tensor"),
        P("expert", None),
        P("expert", None),
        P("tensor", None),
        P("tensor", None),
        P("tensor", None),
        P("expert", "tensor", None),
        P("expert", "tensor", None),
        P("expert", "tensor", None),
    )
    out_specs = (P("expert", "tensor"), P("expert", "tensor"))
    return jax.shard_map(
        on_device, mesh=mesh, in_specs=in_specs, out_specs=out_specs, check_vma=False
    )
```

```python
import functools

import jax
import jax.numpy as jnp
from jax import lax
from jax.experimental import pallas as pl
from jax.experimental.pallas import tpu as pltpu
from jax.sharding import PartitionSpec as P

MESH = pl.DeviceIdType.MESH
F32 = jnp.float32
BF16 = jnp.bfloat16
CAP = 6
Z_SIZE = 8
WIDE = 4
OWN_ROWS = (4, 5)
SIB_ROWS = (0, 1, 2, 3, 4, 5)
NB = len(OWN_ROWS) + len(SIB_ROWS)
NA = 2 * WIDE
NEAR = 3


def nt_dot(a, b):
    return lax.dot_general(a, b, (((1,), (1,)), ((), ())), preferred_element_type=F32)


def nn_dot(a, b):
    return jnp.dot(a, b, preferred_element_type=F32)


def silu_parts(v):
    s = jax.nn.sigmoid(v)
    return v * s, s * (1.0 + v * (1.0 - s))


def slot_ranks(shape, first, ranks):
    i = lax.broadcasted_iota(jnp.int32, shape, 1)
    inside = (i >= first) & (i < first + len(ranks))
    return jnp.where(inside, i - first + ranks[0], -1).astype(F32)


def kernel(
    dims,
    tok,
    cot,
    ids,
    wts,
    sg_h,
    su_h,
    sd_h,
    eg_h,
    eu_h,
    ed_h,
    out_v,
    out_i,
    sg,
    su,
    sd,
    eg,
    eu,
    ed,
    meta_out,
    meta_in,
    sib,
    full,
    b_send,
    b_recv,
    b_full,
    r_out,
    r_in,
    t_out,
    t_in,
    ret_send,
    ret_recv,
    near_send,
    far_send,
    near_recv,
    far_recv,
    near_back,
    far_back,
    near_home,
    far_home,
    fin_out,
    fin_in,
    acc_s,
    acc_b,
    acc_a,
    comb,
    comb_a,
    w_sem,
    sib_send,
    sib_recv,
    ag_send,
    ag_recv,
    rs_send,
    rs_recv,
    a2a_send,
    a2a_recv,
    round_sem,
):
    nq, nx, nz, ny = dims
    t_rows, lanes = tok.shape
    half = ny // 2
    e_me = lax.axis_index("expert")
    y = lax.axis_index("tensor")
    core = e_me % 2
    q = e_me // 2
    x = q // nz
    z = q % nz
    sibling = (e_me + 1 - 2 * core, y)
    sides = ((e_me, (y + 1) % ny), (e_me, (y + ny - 1) % ny))
    pairs = [(kind, way) for kind in range(2) for way in range(2)]
    offsets = [0]
    for s in range(1, half):
        offsets += [-s, s]
    offsets += [half]

    def block_at(off):
        return lax.rem(y + off + ny, ny)

    def at_offset(d, sign):
        dx = lax.div(d, nz) if not isinstance(d, int) else d // nz
        dz = lax.rem(d, nz) if not isinstance(d, int) else d % nz
        xx = lax.rem(x + dx if sign > 0 else x - dx + nx, nx)
        zz = lax.rem(z + dz if sign > 0 else z - dz + nz, nz)
        return (2 * (xx * nz + zz) + core, y)

    def send(src, dst, s_sem, r_sem, dev):
        return pltpu.make_async_remote_copy(
            src_ref=src, dst_ref=dst, send_sem=s_sem, recv_sem=r_sem, device_id=dev, device_id_type=MESH
        )

    def cols(ref, blk):
        return ref[:, pl.ds(pl.multiple_of(blk * lanes, lanes), lanes)]

    barrier = pltpu.get_barrier_semaphore()
    column = [at_offset(k * nz, 1) for k in range(1, nx)]
    greeted = [*sides, sibling, *column, *(at_offset(k, 1) for k in range(1, nz))]
    for dev in greeted:
        pl.semaphore_signal(barrier, inc=1, device_id=dev, device_id_type=MESH)

    loads = [
        pltpu.make_async_copy(h, v, w_sem.at[k])
        for k, (h, v) in enumerate(
            ((sg_h, sg), (su_h, su), (sd_h, sd), (eg_h, eg), (eu_h, eu), (ed_h, ed))
        )
    ]
    for load in loads:
        load.start()

    full[0, y] = tok[...]
    full[1, y] = cot[...]

    def steps_of(kind, way):
        return half if (kind + way) % 2 == 0 else half - 1

    def ag_copy(buf, group, kind, way, s):
        at = buf.at[kind, block_at(-s if way == 0 else s)]
        return send(at, at, ag_send.at[group], ag_recv.at[group, kind, way, s], sides[way])

    def ag_start(buf, group):
        for kind, way in pairs:
            ag_copy(buf, group, kind, way, 0).start()

    def ag_step(buf, group, s):
        for kind, way in pairs:
            ag_copy(buf, group, kind, way, s - 1).wait_recv()
            if s < steps_of(kind, way):
                ag_copy(buf, group, kind, way, s).start()

    def ag_last(buf, group):
        for kind, way in pairs:
            if steps_of(kind, way) == half:
                ag_copy(buf, group, kind, way, half - 1).wait_recv()

    def all_sent(ref, sem):
        pltpu.make_async_copy(ref, ref, sem).wait()

    pl.semaphore_wait(barrier, len(greeted))
    ag_start(full, 0)
    to_sib = [
        send(tok, sib.at[0], sib_send.at[1], sib_recv.at[1], sibling),
        send(cot, sib.at[1], sib_send.at[2], sib_recv.at[2], sibling),
    ]
    for copy in to_sib:
        copy.start()
    for dev in column:
        pl.semaphore_signal(round_sem, inc=1, device_id=dev, device_id_type=MESH)

    line = lax.broadcasted_iota(jnp.int32, (2 * nq, t_rows), 0)
    d_of = line % nq
    xx = (x + d_of // nz) % nx
    zz = (z + d_of % nz) % nz
    e_of = 2 * (xx * nz + zz) + jnp.where(line < nq, core, 1 - core)
    named = jnp.zeros((2 * nq, t_rows), F32)
    weight = jnp.zeros((2 * nq, t_rows), F32)
    for k in range(ids.shape[0]):
        hit = ids[k : k + 1, :] == e_of
        named = named + jnp.where(hit, 1.0, 0.0)
        weight = weight + jnp.where(hit, wts[k : k + 1, :], 0.0)
    row = lax.broadcasted_iota(jnp.int32, (t_rows, t_rows), 0)
    col = lax.broadcasted_iota(jnp.int32, (t_rows, t_rows), 1)
    before = jnp.where(row < col, 1.0, 0.0).astype(BF16)
    rank = jnp.where(named > 0.0, nn_dot(named.astype(BF16), before), 1000.0)
    meta_out[0] = rank[nq:]
    meta_out[1] = weight[nq:]

    to_sib.append(send(meta_out, meta_in, sib_send.at[0], sib_recv.at[0], sibling))
    to_sib[2].start()

    def first_layer(acc, v, g, weights, blk, first):
        gate, up, down = weights
        for k, (rows, w) in enumerate(((v, gate), (v, up), (g, down))):
            term = nt_dot(rows, cols(w, blk))
            acc[k] = term if first else acc[k] + term

    def shared_first(off):
        blk = block_at(off)
        first_layer(acc_s, full[0, blk], full[1, blk], (sg, su, sd), blk, off == 0)

    def routed_first(h, off):
        blk = block_at(off)
        first_layer(acc_b.at[h], b_full[h, 0, blk], b_full[h, 1, blk], (eg, eu, ed), blk, off == 0)

    shape = (nq, NB, t_rows)
    own_rank = slot_ranks(shape, 0, OWN_ROWS)
    sib_rank = slot_ranks(shape, len(OWN_ROWS), SIB_ROWS)

    def place(rank_rows, weight_rows, wanted):
        n = wanted.shape[1]
        pick = jnp.where(rank_rows.reshape(nq, 1, t_rows) == wanted, 1.0, 0.0)
        scaled = pick * weight_rows.reshape(nq, 1, t_rows)
        return pick.reshape(nq * n, t_rows), scaled.reshape(nq * n, t_rows)

    own_pick, own_scaled = place(rank[:nq], weight[:nq], own_rank)
    ag_step(full, 0, 1)
    for copy in to_sib:
        copy.wait_recv()
    sib_pick, sib_scaled = place(meta_in[0], meta_in[1], sib_rank)
    slot_weight = jnp.sum(own_scaled, axis=1, keepdims=True) + jnp.sum(sib_scaled, axis=1, keepdims=True)
    own_bf, sib_bf = own_pick.astype(BF16), sib_pick.astype(BF16)
    x_rows = nn_dot(own_bf, tok[...]) + nn_dot(sib_bf, sib[0])
    g_rows = slot_weight * (nn_dot(own_bf, cot[...]) + nn_dot(sib_bf, sib[1]))
    slabs = jnp.concatenate((x_rows.reshape(nq, NB, lanes), g_rows.reshape(nq, NB, lanes)), axis=1)
    b_send[...] = slabs.astype(BF16)

    mid = nq // 2
    swaps = []

    class Swap:
        def __init__(self, src, dst, sign, first=1, last=nq):
            self.k = len(swaps)
            self.src, self.dst, self.sign, self.first, self.last = src, dst, sign, first, last
            swaps.append(self)

        def start(self, first=None, last=None):
            @pl.loop(self.first if first is None else first, self.last if last is None else last)
            def _(d):
                dev = at_offset(d, self.sign)
                send(self.src.at[d], self.dst.at[d], a2a_send.at[self.k], a2a_recv.at[self.k], dev).start()

        def part(self, ref):
            return ref.at[pl.ds(self.first, self.last - self.first)]

        def wait(self):
            all_sent(self.part(self.dst), a2a_recv.at[self.k])

        def end(self):
            all_sent(self.part(self.src), a2a_send.at[self.k])

    b_out = [Swap(b_send, b_recv, 1, max(1, h * mid), (h + 1) * mid) for h in range(2)]
    near_out = Swap(near_send, near_recv, 1)
    far_out = Swap(far_send, far_recv, 1)
    far_in = Swap(far_back, far_home, -1)
    near_in = Swap(near_back, near_home, -1)
    b_in = [Swap(ret_send, ret_recv, -1, max(1, h * mid), (h + 1) * mid) for h in range(2)]

    if nx > 1:
        pl.semaphore_wait(round_sem, nx - 1)
    b_out[0].start()
    if half > 2:
        ag_step(full, 0, 2)
    b_out[1].start()
    b_recv[0] = b_send[0]

    slot = lax.broadcasted_iota(jnp.int32, (nq, NA, t_rows), 1)
    wide_rank = jnp.where(slot < WIDE, slot, slot - WIDE).astype(F32)
    wide_pick, wide_scaled = place(rank[:nq], weight[:nq], wide_rank)
    slot = slot.reshape(nq * NA, t_rows)
    top = slot < WIDE
    x_pick = jnp.where(top, wide_pick, 0.0).astype(BF16)
    g_pick = jnp.where(top, 0.0, wide_pick).astype(BF16)
    slot = lax.broadcasted_iota(jnp.int32, (nq, NA, 1), 1).reshape(nq * NA, 1)
    row_scale = jnp.where(slot < WIDE, 1.0, jnp.sum(wide_scaled, axis=1, keepdims=True))

    def wide_rows(p):
        blk = block_at(offsets[p])
        rows = row_scale * (nn_dot(x_pick, full[0, blk]) + nn_dot(g_pick, full[1, blk]))
        rows = rows.reshape(nq, NA, lanes).astype(BF16)
        if p < NEAR:
            near_send[:, :, p * lanes : (p + 1) * lanes] = rows
        else:
            far_send[:, :, (p - NEAR) * lanes : (p - NEAR + 1) * lanes] = rows

    def unpack_slabs(ref, h):
        v = ref[h * mid : (h + 1) * mid].astype(F32)
        return [v[:, k * NB : (k + 1) * NB].reshape(mid * NB, lanes) for k in range(2)]

    for p in range(NEAR):
        wide_rows(p)
    for s in range(3, half):
        ag_step(full, 0, s)
    for h in range(2):
        b_out[h].wait()
        for kind, v in enumerate(unpack_slabs(b_recv, h)):
            b_full[h, kind, y] = v.astype(BF16)
        ag_start(b_full.at[h], 1 + h)
        near_out.start(max(1, h * mid), (h + 1) * mid)
    near_recv[0] = near_send[0]
    ag_last(full, 0)
    for p in range(NEAR, ny):
        wide_rows(p)
    far_recv[0] = far_send[0]

    def middle(gate, up, grad):
        act, slope = silu_parts(gate)
        return (
            (act * up).astype(BF16),
            (grad * up * slope).astype(BF16),
            (grad * act).astype(BF16),
        )

    def second_layer(mid, weights):
        hidden, grad_gate, grad_up = mid
        gate, up, down = weights

        def of(kind, blk):
            if kind == 0:
                return nn_dot(hidden, cols(down, blk))
            return nn_dot(grad_gate, cols(gate, blk)) + nn_dot(grad_up, cols(up, blk))

        return of

    for load in loads:
        load.wait()
    def take_wide(p):
        ref, at = (near_recv, p) if p < NEAR else (far_recv, p - NEAR)
        v = ref[:, :, at * lanes : (at + 1) * lanes].astype(F32).reshape(nq * NA, lanes).astype(BF16)
        first_layer(acc_a, v, v, (eg, eu, ed), block_at(offsets[p]), p == 0)

    todo = list(offsets)
    turns = [(s, h) for s in range(1, half) for h in range(2)]
    for n, (s, h) in enumerate(turns):
        ag_step(b_full.at[h], 1 + h, s)
        if n < 2:
            far_out.start(max(1, n * mid), (n + 1) * mid)
        for off in ([0] if s == 1 else []) + [-s, s]:
            routed_first(h, off)
        share = -(-len(todo) // (len(turns) - n))
        for off in todo[:share]:
            shared_first(off)
        todo = todo[share:]
    shared_mid = middle(acc_s[0], acc_s[1], acc_s[2])

    def rs_offset(kind, way, s):
        far = steps_of(kind, way) - s
        return far if way == 0 else -far

    def rs_copy(o, i, group, kind, way, s):
        return send(
            o.at[kind, way, s],
            i.at[kind, way, s],
            rs_send.at[group],
            rs_recv.at[group, kind, way, s],
            sides[way],
        )

    def rs_step(o, i, group, s, compute):
        for kind, way in pairs:
            if s < steps_of(kind, way):
                term = compute(kind, rs_offset(kind, way, s))
                if s > 0:
                    rs_copy(o, i, group, kind, way, s - 1).wait_recv()
                    term = term + i[kind, way, s - 1].astype(F32)
                o[kind, way, s] = term.astype(BF16)
                rs_copy(o, i, group, kind, way, s).start()

    def rs_total(o, i, group, compute):
        totals = []
        for kind in range(2):
            total = compute(kind, 0)
            for way in range(2):
                n = steps_of(kind, way)
                rs_copy(o, i, group, kind, way, n - 1).wait_recv()
                total = total + i[kind, way, n - 1].astype(F32)
            totals.append(total)
        return totals

    second_b = []

    def routed_term(h):
        return lambda kind, off: second_b[h](kind, block_at(off))

    def routed_step(h, s):
        rs_step(r_out.at[h], r_in.at[h], 1 + h, s, routed_term(h))

    for h in range(2):
        ag_last(b_full.at[h], 1 + h)
        routed_first(h, half)
        second_b.append(second_layer(middle(acc_b[h, 0], acc_b[h, 1], acc_b[h, 2]), (eg, eu, ed)))
        routed_step(h, 0)

    near_out.wait()
    for p in range(NEAR):
        take_wide(p)
    far_out.wait()
    for p in range(NEAR, ny):
        take_wide(p)
    routed_step(0, 1)
    hid = sg.shape[0]
    slot = lax.broadcasted_iota(jnp.int32, (nq, NA, hid), 1).reshape(nq * NA, hid)
    top_hid = slot < WIDE
    gate_a, up_a = acc_a[0], acc_a[1]
    act, slope = silu_parts(gate_a)
    hidden_a = jnp.where(top_hid, act * up_a, 0.0).astype(BF16)

    def lowered(v):
        v = v.reshape(nq, NA, hid)
        return jnp.concatenate((v[:, WIDE:], v[:, :WIDE]), axis=1).reshape(nq * NA, hid)

    grad_a = acc_a[2]
    grad_gate_a = jnp.where(top_hid, 0.0, grad_a * lowered(up_a) * lowered(slope)).astype(BF16)
    grad_up_a = jnp.where(top_hid, 0.0, grad_a * lowered(act)).astype(BF16)
    wide_second = second_layer((hidden_a, grad_gate_a, grad_up_a), (eg, eu, ed))

    def wide_back(p):
        blk = block_at(offsets[p])
        rows = (wide_second(0, blk) + wide_second(1, blk)).reshape(nq, NA, lanes).astype(BF16)
        if p < NEAR:
            near_back[:, :, p * lanes : (p + 1) * lanes] = rows
        else:
            far_back[:, :, (p - NEAR) * lanes : (p - NEAR + 1) * lanes] = rows

    for p in range(NEAR, ny):
        wide_back(p)
    far_in.start(1, mid)
    routed_step(1, 1)
    far_in.start(mid, nq)
    far_home[0] = far_back[0]
    for p in range(NEAR):
        wide_back(p)
    near_home[0] = near_back[0]
    for s in range(2, half):
        for h in range(2):
            routed_step(h, s)
            if s == 2:
                near_in.start(max(1, h * mid), (h + 1) * mid)
    if half < 3:
        near_in.start()

    for k, (pick, scaled) in enumerate(((own_pick, own_scaled), (sib_pick, sib_scaled))):
        high = scaled.astype(BF16).astype(F32)
        comb[k, 0] = pick.T.astype(BF16)
        comb[k, 1] = high.T.astype(BF16)
        comb[k, 2] = (scaled - high).T.astype(BF16)
    wide_scaled = jnp.where(top, wide_scaled, 0.0)
    high = wide_scaled.astype(BF16).astype(F32)
    comb_a[0] = jnp.where(top, 0.0, wide_pick).T.astype(BF16)
    comb_a[1] = high.T.astype(BF16)
    comb_a[2] = (wide_scaled - high).T.astype(BF16)

    shared_second = second_layer(shared_mid, (sg, su, sd))

    def token_term(kind, off):
        p = offsets.index(off if -off != half else half)
        home, at = (near_home, p) if p < NEAR else (far_home, p - NEAR)
        rows = home[:, :, at * lanes : (at + 1) * lanes]
        rows = rows.astype(F32).reshape(nq * NA, lanes).astype(BF16)
        total = shared_second(kind, block_at(off))
        if kind == 0:
            return total + nn_dot(comb_a[1], rows) + nn_dot(comb_a[2], rows)
        return total + nn_dot(comb_a[0], rows)

    def send_home(h):
        pair = rs_total(r_out.at[h], r_in.at[h], 1 + h, routed_term(h))
        slabs = jnp.concatenate([v.reshape(mid, NB, lanes) for v in pair], axis=1)
        ret_send[h * mid : (h + 1) * mid] = slabs.astype(BF16)
        b_in[h].start()

    send_home(0)
    near_from = half - 2
    far_in.wait()
    for s in range(half):
        if s == near_from:
            near_in.wait()
        rs_step(t_out, t_in, 0, s, token_term)
        if s == 0:
            send_home(1)
            ret_recv[0] = ret_send[0]

    for swap in b_in:
        swap.wait()
    halves = [unpack_slabs(ret_recv, h) for h in range(2)]
    value_r, input_r = (jnp.concatenate([v[k] for v in halves], axis=0).astype(BF16) for k in range(2))

    fin_out[0] = nn_dot(comb[1, 1], value_r) + nn_dot(comb[1, 2], value_r)
    fin_out[1] = nn_dot(comb[1, 0], input_r)
    last = send(fin_out, fin_in, sib_send.at[3], sib_recv.at[3], sibling)
    last.start()
    value_t, input_t = rs_total(t_out, t_in, 0, token_term)
    value_t = value_t + nn_dot(comb[0, 1], value_r) + nn_dot(comb[0, 2], value_r)
    input_t = input_t + nn_dot(comb[0, 0], input_r)
    last.wait_recv()
    out_v[...] = (value_t + fin_in[0]).astype(out_v.dtype)
    out_i[...] = (input_t + fin_in[1]).astype(out_i.dtype)

    for group, buf in enumerate((full, b_full.at[0], b_full.at[1])):
        sent = buf.at[:, pl.ds(0, ny - 1)]
        all_sent(sent, ag_send.at[group])
        all_sent(sent, rs_send.at[group])
    for copy in (*to_sib, last):
        copy.wait_send()
    for swap in swaps:
        swap.end()


def on_device(*args):
    tokens, cotangent, route_ids, route_weights, sg, su, sd, eg, eu, ed = args
    ny = lax.axis_size("tensor")
    nq = lax.axis_size("expert") // 2
    nz = min(Z_SIZE, nq)
    t_rows, lanes = tokens.shape
    hid, feats = sg.shape
    half = ny // 2
    eg, eu, ed = (w.reshape(hid, feats) for w in (eg, eu, ed))
    rows = nq * NB
    vmem, dma = pltpu.VMEM, pltpu.SemaphoreType.DMA
    out = jax.ShapeDtypeStruct((t_rows, lanes), BF16)
    in_vmem = pl.BlockSpec(memory_space=pltpu.VMEM)
    in_any = pl.BlockSpec(memory_space=pl.ANY)
    return pl.pallas_call(
        functools.partial(kernel, (nq, nq // nz, nz, ny)),
        out_shape=(out, out),
        in_specs=[in_vmem] * 4 + [in_any] * 6,
        out_specs=(in_vmem, in_vmem),
        scratch_shapes=[
            *[vmem((hid, feats), BF16)] * 6,
            vmem((2, nq, t_rows), F32),
            vmem((2, nq, t_rows), F32),
            vmem((2, t_rows, lanes), BF16),
            vmem((2, ny, t_rows, lanes), BF16),
            vmem((nq, 2 * NB, lanes), BF16),
            vmem((nq, 2 * NB, lanes), BF16),
            vmem((2, 2, ny, rows // 2, lanes), BF16),
            vmem((2, 2, 2, half, rows // 2, lanes), BF16),
            vmem((2, 2, 2, half, rows // 2, lanes), BF16),
            vmem((2, 2, half, t_rows, lanes), BF16),
            vmem((2, 2, half, t_rows, lanes), BF16),
            vmem((nq, 2 * NB, lanes), BF16),
            vmem((nq, 2 * NB, lanes), BF16),
            *[vmem((nq, NA, n * lanes), BF16) for n in (NEAR, ny - NEAR)] * 4,
            vmem((2, t_rows, lanes), F32),
            vmem((2, t_rows, lanes), F32),
            vmem((3, t_rows, hid), F32),
            vmem((2, 3, rows // 2, hid), F32),
            vmem((3, nq * NA, hid), F32),
            vmem((2, 3, t_rows, rows), BF16),
            vmem((3, t_rows, nq * NA), BF16),
            dma((6,)),
            dma((4,)),
            dma((4,)),
            dma((3,)),
            dma((3, 2, 2, half)),
            dma((3,)),
            dma((3, 2, 2, half)),
            dma((8,)),
            dma((8,)),
            pltpu.SemaphoreType.REGULAR,
        ],
        compiler_params=pltpu.CompilerParams(
            collective_id=0, has_side_effects=True, vmem_limit_bytes=56 * 2**20
        ),
        name="routed_layer",
    )(tokens, cotangent, route_ids.T, route_weights.T, sg, su, sd, eg, eu, ed)


def solution(mesh):
    in_specs = (
        P("expert", "tensor"),
        P("expert", "tensor"),
        P("expert", None),
        P("expert", None),
        P("tensor", None),
        P("tensor", None),
        P("tensor", None),
        P("expert", "tensor", None),
        P("expert", "tensor", None),
        P("expert", "tensor", None),
    )
    out_specs = (P("expert", "tensor"), P("expert", "tensor"))
    return jax.shard_map(
        on_device, mesh=mesh, in_specs=in_specs, out_specs=out_specs, check_vma=False
    )
```

```python
import functools

import jax
import jax.numpy as jnp
from jax import lax
from jax.experimental import pallas as pl
from jax.experimental.pallas import tpu as pltpu
from jax.sharding import PartitionSpec as P

MESH = pl.DeviceIdType.MESH
F32 = jnp.float32
BF16 = jnp.bfloat16
CAP = 6
Z_SIZE = 8
WIDE = 4
OWN_ROWS = (4, 5)
SIB_ROWS = (0, 1, 2, 3, 4, 5)
NB = len(OWN_ROWS) + len(SIB_ROWS)
NA = 2 * WIDE
NEAR = 3


def nt_dot(a, b):
    return lax.dot_general(a, b, (((1,), (1,)), ((), ())), preferred_element_type=F32)


def nn_dot(a, b):
    return jnp.dot(a, b, preferred_element_type=F32)


def silu_parts(v):
    s = jax.nn.sigmoid(v)
    return v * s, s * (1.0 + v * (1.0 - s))


def slot_ranks(shape, first, ranks):
    i = lax.broadcasted_iota(jnp.int32, shape, 1)
    inside = (i >= first) & (i < first + len(ranks))
    return jnp.where(inside, i - first + ranks[0], -1).astype(F32)


def kernel(
    dims,
    tok,
    cot,
    ids,
    wts,
    sg_h,
    su_h,
    sd_h,
    eg_h,
    eu_h,
    ed_h,
    out_v,
    out_i,
    sg,
    su,
    sd,
    eg,
    eu,
    ed,
    meta_out,
    meta_in,
    sib,
    full,
    b_send,
    b_recv,
    b_full,
    r_out,
    r_in,
    t_out,
    t_in,
    ret_send,
    ret_recv,
    near_send,
    far_send,
    near_recv,
    far_recv,
    near_back,
    far_back,
    near_home,
    far_home,
    fin_out,
    fin_in,
    acc_s,
    acc_b,
    acc_a,
    comb,
    comb_a,
    w_sem,
    sib_send,
    sib_recv,
    ag_send,
    ag_recv,
    rs_send,
    rs_recv,
    a2a_send,
    a2a_recv,
    round_sem,
):
    nq, nx, nz, ny = dims
    t_rows, lanes = tok.shape
    half = ny // 2
    e_me = lax.axis_index("expert")
    y = lax.axis_index("tensor")
    core = e_me % 2
    q = e_me // 2
    x = q // nz
    z = q % nz
    sibling = (e_me + 1 - 2 * core, y)
    sides = ((e_me, (y + 1) % ny), (e_me, (y + ny - 1) % ny))
    pairs = [(kind, way) for kind in range(2) for way in range(2)]
    offsets = [0]
    for s in range(1, half):
        offsets += [-s, s]
    offsets += [half]

    def block_at(off):
        return lax.rem(y + off + ny, ny)

    def at_offset(d, sign):
        dx = lax.div(d, nz) if not isinstance(d, int) else d // nz
        dz = lax.rem(d, nz) if not isinstance(d, int) else d % nz
        xx = lax.rem(x + dx if sign > 0 else x - dx + nx, nx)
        zz = lax.rem(z + dz if sign > 0 else z - dz + nz, nz)
        return (2 * (xx * nz + zz) + core, y)

    def send(src, dst, s_sem, r_sem, dev):
        return pltpu.make_async_remote_copy(
            src_ref=src, dst_ref=dst, send_sem=s_sem, recv_sem=r_sem, device_id=dev, device_id_type=MESH
        )

    def cols(ref, blk):
        return ref[:, pl.ds(pl.multiple_of(blk * lanes, lanes), lanes)]

    barrier = pltpu.get_barrier_semaphore()
    column = [at_offset(k * nz, 1) for k in range(1, nx)]
    greeted = [*sides, sibling, *column, *(at_offset(k, 1) for k in range(1, nz))]
    for dev in greeted:
        pl.semaphore_signal(barrier, inc=1, device_id=dev, device_id_type=MESH)

    loads = [
        pltpu.make_async_copy(h, v, w_sem.at[k])
        for k, (h, v) in enumerate(
            ((sg_h, sg), (su_h, su), (sd_h, sd), (eg_h, eg), (eu_h, eu), (ed_h, ed))
        )
    ]
    for load in loads:
        load.start()

    full[0, y] = tok[...]
    full[1, y] = cot[...]

    def steps_of(kind, way):
        return half if (kind + way) % 2 == 0 else half - 1

    def ag_copy(buf, group, kind, way, s):
        at = buf.at[kind, block_at(-s if way == 0 else s)]
        return send(at, at, ag_send.at[group], ag_recv.at[group, kind, way, s], sides[way])

    def ag_start(buf, group):
        for kind, way in pairs:
            ag_copy(buf, group, kind, way, 0).start()

    def ag_step(buf, group, s):
        for kind, way in pairs:
            ag_copy(buf, group, kind, way, s - 1).wait_recv()
            if s < steps_of(kind, way):
                ag_copy(buf, group, kind, way, s).start()

    def ag_last(buf, group):
        for kind, way in pairs:
            if steps_of(kind, way) == half:
                ag_copy(buf, group, kind, way, half - 1).wait_recv()

    def all_sent(ref, sem):
        pltpu.make_async_copy(ref, ref, sem).wait()

    pl.semaphore_wait(barrier, len(greeted))
    ag_start(full, 0)
    to_sib = [
        send(tok, sib.at[0], sib_send.at[1], sib_recv.at[1], sibling),
        send(cot, sib.at[1], sib_send.at[2], sib_recv.at[2], sibling),
    ]
    for copy in to_sib:
        copy.start()
    for dev in column:
        pl.semaphore_signal(round_sem, inc=1, device_id=dev, device_id_type=MESH)

    line = lax.broadcasted_iota(jnp.int32, (2 * nq, t_rows), 0)
    d_of = line % nq
    xx = (x + d_of // nz) % nx
    zz = (z + d_of % nz) % nz
    e_of = 2 * (xx * nz + zz) + jnp.where(line < nq, core, 1 - core)
    named = jnp.zeros((2 * nq, t_rows), F32)
    weight = jnp.zeros((2 * nq, t_rows), F32)
    for k in range(ids.shape[0]):
        hit = ids[k : k + 1, :] == e_of
        named = named + jnp.where(hit, 1.0, 0.0)
        weight = weight + jnp.where(hit, wts[k : k + 1, :], 0.0)
    row = lax.broadcasted_iota(jnp.int32, (t_rows, t_rows), 0)
    col = lax.broadcasted_iota(jnp.int32, (t_rows, t_rows), 1)
    before = jnp.where(row < col, 1.0, 0.0).astype(BF16)
    rank = jnp.where(named > 0.0, nn_dot(named.astype(BF16), before), 1000.0)
    meta_out[0] = rank[nq:]
    meta_out[1] = weight[nq:]

    to_sib.append(send(meta_out, meta_in, sib_send.at[0], sib_recv.at[0], sibling))
    to_sib[2].start()

    def first_layer(acc, v, g, weights, blk, first):
        gate, up, down = weights
        for k, (rows, w) in enumerate(((v, gate), (v, up), (g, down))):
            term = nt_dot(rows, cols(w, blk))
            acc[k] = term if first else acc[k] + term

    def shared_first(off):
        blk = block_at(off)
        first_layer(acc_s, full[0, blk], full[1, blk], (sg, su, sd), blk, off == 0)

    def routed_first(h, off):
        blk = block_at(off)
        first_layer(acc_b.at[h], b_full[h, 0, blk], b_full[h, 1, blk], (eg, eu, ed), blk, off == 0)

    shape = (nq, NB, t_rows)
    own_rank = slot_ranks(shape, 0, OWN_ROWS)
    sib_rank = slot_ranks(shape, len(OWN_ROWS), SIB_ROWS)

    def place(rank_rows, weight_rows, wanted):
        n = wanted.shape[1]
        pick = jnp.where(rank_rows.reshape(nq, 1, t_rows) == wanted, 1.0, 0.0)
        scaled = pick * weight_rows.reshape(nq, 1, t_rows)
        return pick.reshape(nq * n, t_rows), scaled.reshape(nq * n, t_rows)

    own_pick, own_scaled = place(rank[:nq], weight[:nq], own_rank)
    ag_step(full, 0, 1)
    for copy in to_sib:
        copy.wait_recv()
    sib_pick, sib_scaled = place(meta_in[0], meta_in[1], sib_rank)
    slot_weight = jnp.sum(own_scaled, axis=1, keepdims=True) + jnp.sum(sib_scaled, axis=1, keepdims=True)
    own_bf, sib_bf = own_pick.astype(BF16), sib_pick.astype(BF16)
    x_rows = nn_dot(own_bf, tok[...]) + nn_dot(sib_bf, sib[0])
    g_rows = slot_weight * (nn_dot(own_bf, cot[...]) + nn_dot(sib_bf, sib[1]))
    slabs = jnp.concatenate((x_rows.reshape(nq, NB, lanes), g_rows.reshape(nq, NB, lanes)), axis=1)
    b_send[...] = slabs.astype(BF16)

    mid = nq // 2
    swaps = []

    class Swap:
        def __init__(self, src, dst, sign, first=1, last=nq):
            self.k = len(swaps)
            self.src, self.dst, self.sign, self.first, self.last = src, dst, sign, first, last
            swaps.append(self)

        def start(self, first=None, last=None):
            @pl.loop(self.first if first is None else first, self.last if last is None else last)
            def _(d):
                dev = at_offset(d, self.sign)
                send(self.src.at[d], self.dst.at[d], a2a_send.at[self.k], a2a_recv.at[self.k], dev).start()

        def part(self, ref):
            return ref.at[pl.ds(self.first, self.last - self.first)]

        def wait(self):
            all_sent(self.part(self.dst), a2a_recv.at[self.k])

        def end(self):
            all_sent(self.part(self.src), a2a_send.at[self.k])

    b_out = [Swap(b_send, b_recv, 1, max(1, h * mid), (h + 1) * mid) for h in range(2)]
    near_out = Swap(near_send, near_recv, 1)
    far_out = Swap(far_send, far_recv, 1)
    far_in = Swap(far_back, far_home, -1)
    near_in = Swap(near_back, near_home, -1)
    b_in = [Swap(ret_send, ret_recv, -1, max(1, h * mid), (h + 1) * mid) for h in range(2)]

    if nx > 1:
        pl.semaphore_wait(round_sem, nx - 1)
    b_out[0].start()
    if half > 2:
        ag_step(full, 0, 2)
    b_out[1].start()
    b_recv[0] = b_send[0]

    slot = lax.broadcasted_iota(jnp.int32, (nq, NA, t_rows), 1)
    wide_rank = jnp.where(slot < WIDE, slot, slot - WIDE).astype(F32)
    wide_pick, wide_scaled = place(rank[:nq], weight[:nq], wide_rank)
    slot = slot.reshape(nq * NA, t_rows)
    top = slot < WIDE
    x_pick = jnp.where(top, wide_pick, 0.0).astype(BF16)
    g_pick = jnp.where(top, 0.0, wide_pick).astype(BF16)
    slot = lax.broadcasted_iota(jnp.int32, (nq, NA, 1), 1).reshape(nq * NA, 1)
    row_scale = jnp.where(slot < WIDE, 1.0, jnp.sum(wide_scaled, axis=1, keepdims=True))

    def wide_rows(p):
        blk = block_at(offsets[p])
        rows = row_scale * (nn_dot(x_pick, full[0, blk]) + nn_dot(g_pick, full[1, blk]))
        rows = rows.reshape(nq, NA, lanes).astype(BF16)
        if p < NEAR:
            near_send[:, :, p * lanes : (p + 1) * lanes] = rows
        else:
            far_send[:, :, (p - NEAR) * lanes : (p - NEAR + 1) * lanes] = rows

    def unpack_slabs(ref, h):
        v = ref[h * mid : (h + 1) * mid].astype(F32)
        return [v[:, k * NB : (k + 1) * NB].reshape(mid * NB, lanes) for k in range(2)]

    for p in range(NEAR):
        wide_rows(p)
    near_out.start(1, mid)
    for s in range(3, half):
        ag_step(full, 0, s)
    near_out.start(mid, nq)
    for h in range(2):
        b_out[h].wait()
        for kind, v in enumerate(unpack_slabs(b_recv, h)):
            b_full[h, kind, y] = v.astype(BF16)
        ag_start(b_full.at[h], 1 + h)
    near_recv[0] = near_send[0]
    ag_last(full, 0)
    for p in range(NEAR, ny):
        wide_rows(p)
    far_recv[0] = far_send[0]
    far_out.start(1, mid)

    def middle(gate, up, grad):
        act, slope = silu_parts(gate)
        return (
            (act * up).astype(BF16),
            (grad * up * slope).astype(BF16),
            (grad * act).astype(BF16),
        )

    def second_layer(mid, weights):
        hidden, grad_gate, grad_up = mid
        gate, up, down = weights

        def of(kind, blk):
            if kind == 0:
                return nn_dot(hidden, cols(down, blk))
            return nn_dot(grad_gate, cols(gate, blk)) + nn_dot(grad_up, cols(up, blk))

        return of

    for load in loads:
        load.wait()
    def take_wide(p):
        ref, at = (near_recv, p) if p < NEAR else (far_recv, p - NEAR)
        v = ref[:, :, at * lanes : (at + 1) * lanes].astype(F32).reshape(nq * NA, lanes).astype(BF16)
        first_layer(acc_a, v, v, (eg, eu, ed), block_at(offsets[p]), p == 0)

    todo = list(offsets)
    turns = [(s, h) for s in range(1, half) for h in range(2)]
    for n, (s, h) in enumerate(turns):
        ag_step(b_full.at[h], 1 + h, s)
        if n == 1:
            far_out.start(mid, nq)
        if n == len(turns) - 1:
            near_out.wait()
            for p in range(NEAR):
                take_wide(p)
        for off in ([0] if s == 1 else []) + [-s, s]:
            routed_first(h, off)
        share = -(-len(todo) // (len(turns) - n))
        for off in todo[:share]:
            shared_first(off)
        todo = todo[share:]
    shared_mid = middle(acc_s[0], acc_s[1], acc_s[2])

    def rs_offset(kind, way, s):
        far = steps_of(kind, way) - s
        return far if way == 0 else -far

    def rs_copy(o, i, group, kind, way, s):
        return send(
            o.at[kind, way, s],
            i.at[kind, way, s],
            rs_send.at[group],
            rs_recv.at[group, kind, way, s],
            sides[way],
        )

    def rs_step(o, i, group, s, compute):
        for kind, way in pairs:
            if s < steps_of(kind, way):
                term = compute(kind, rs_offset(kind, way, s))
                if s > 0:
                    rs_copy(o, i, group, kind, way, s - 1).wait_recv()
                    term = term + i[kind, way, s - 1].astype(F32)
                o[kind, way, s] = term.astype(BF16)
                rs_copy(o, i, group, kind, way, s).start()

    def rs_total(o, i, group, compute):
        totals = [compute(kind, 0) for kind in range(2)]
        for kind, way in pairs:
            n = steps_of(kind, way)
            rs_copy(o, i, group, kind, way, n - 1).wait_recv()
            totals[kind] = totals[kind] + i[kind, way, n - 1].astype(F32)
        return totals

    second_b = []

    def routed_term(h):
        return lambda kind, off: second_b[h](kind, block_at(off))

    def routed_step(h, s):
        rs_step(r_out.at[h], r_in.at[h], 1 + h, s, routed_term(h))

    for h in range(2):
        ag_last(b_full.at[h], 1 + h)
        routed_first(h, half)
        second_b.append(second_layer(middle(acc_b[h, 0], acc_b[h, 1], acc_b[h, 2]), (eg, eu, ed)))
        routed_step(h, 0)

    far_out.wait()
    for p in range(NEAR, ny):
        take_wide(p)
    hid = sg.shape[0]
    slot = lax.broadcasted_iota(jnp.int32, (nq, NA, hid), 1).reshape(nq * NA, hid)
    top_hid = slot < WIDE
    gate_a, up_a = acc_a[0], acc_a[1]
    act, slope = silu_parts(gate_a)
    hidden_a = jnp.where(top_hid, act * up_a, 0.0).astype(BF16)

    def lowered(v):
        v = v.reshape(nq, NA, hid)
        return jnp.concatenate((v[:, WIDE:], v[:, :WIDE]), axis=1).reshape(nq * NA, hid)

    grad_a = acc_a[2]
    grad_gate_a = jnp.where(top_hid, 0.0, grad_a * lowered(up_a) * lowered(slope)).astype(BF16)
    grad_up_a = jnp.where(top_hid, 0.0, grad_a * lowered(act)).astype(BF16)
    wide_second = second_layer((hidden_a, grad_gate_a, grad_up_a), (eg, eu, ed))

    def wide_back(p):
        blk = block_at(offsets[p])
        rows = (wide_second(0, blk) + wide_second(1, blk)).reshape(nq, NA, lanes).astype(BF16)
        if p < NEAR:
            near_back[:, :, p * lanes : (p + 1) * lanes] = rows
        else:
            far_back[:, :, (p - NEAR) * lanes : (p - NEAR + 1) * lanes] = rows

    for p in range(NEAR, ny):
        wide_back(p)
    far_in.start(1, mid)
    routed_step(0, 1)
    far_in.start(mid, nq)
    far_home[0] = far_back[0]
    routed_step(1, 1)
    for p in range(NEAR):
        wide_back(p)
    near_home[0] = near_back[0]
    for s in range(2, half):
        for h in range(2):
            routed_step(h, s)
            if s == 2:
                near_in.start(max(1, h * mid), (h + 1) * mid)
    if half < 3:
        near_in.start()

    for k, (pick, scaled) in enumerate(((own_pick, own_scaled), (sib_pick, sib_scaled))):
        high = scaled.astype(BF16).astype(F32)
        comb[k, 0] = pick.T.astype(BF16)
        comb[k, 1] = high.T.astype(BF16)
        comb[k, 2] = (scaled - high).T.astype(BF16)
    wide_scaled = jnp.where(top, wide_scaled, 0.0)
    high = wide_scaled.astype(BF16).astype(F32)
    comb_a[0] = jnp.where(top, 0.0, wide_pick).T.astype(BF16)
    comb_a[1] = high.T.astype(BF16)
    comb_a[2] = (wide_scaled - high).T.astype(BF16)

    shared_second = second_layer(shared_mid, (sg, su, sd))

    def token_term(kind, off):
        p = offsets.index(off if -off != half else half)
        home, at = (near_home, p) if p < NEAR else (far_home, p - NEAR)
        rows = home[:, :, at * lanes : (at + 1) * lanes]
        rows = rows.astype(F32).reshape(nq * NA, lanes).astype(BF16)
        total = shared_second(kind, block_at(off))
        if kind == 0:
            return total + nn_dot(comb_a[1], rows) + nn_dot(comb_a[2], rows)
        return total + nn_dot(comb_a[0], rows)

    def send_home(h):
        pair = rs_total(r_out.at[h], r_in.at[h], 1 + h, routed_term(h))
        slabs = jnp.concatenate([v.reshape(mid, NB, lanes) for v in pair], axis=1)
        ret_send[h * mid : (h + 1) * mid] = slabs.astype(BF16)
        b_in[h].start()

    send_home(0)
    near_from = half - 2
    far_in.wait()
    for s in range(half):
        if s == near_from:
            near_in.wait()
        rs_step(t_out, t_in, 0, s, token_term)
        if s == 0:
            send_home(1)
            ret_recv[0] = ret_send[0]

    for swap in b_in:
        swap.wait()
    halves = [unpack_slabs(ret_recv, h) for h in range(2)]
    value_r, input_r = (jnp.concatenate([v[k] for v in halves], axis=0).astype(BF16) for k in range(2))

    fin_out[0] = nn_dot(comb[1, 1], value_r) + nn_dot(comb[1, 2], value_r)
    fin_out[1] = nn_dot(comb[1, 0], input_r)
    last = send(fin_out, fin_in, sib_send.at[3], sib_recv.at[3], sibling)
    last.start()
    value_t, input_t = rs_total(t_out, t_in, 0, token_term)
    value_t = value_t + nn_dot(comb[0, 1], value_r) + nn_dot(comb[0, 2], value_r)
    input_t = input_t + nn_dot(comb[0, 0], input_r)
    last.wait_recv()
    out_v[...] = (value_t + fin_in[0]).astype(out_v.dtype)
    out_i[...] = (input_t + fin_in[1]).astype(out_i.dtype)

    for group, buf in enumerate((full, b_full.at[0], b_full.at[1])):
        sent = buf.at[:, pl.ds(0, ny - 1)]
        all_sent(sent, ag_send.at[group])
        all_sent(sent, rs_send.at[group])
    for copy in (*to_sib, last):
        copy.wait_send()
    for swap in swaps:
        swap.end()


def on_device(*args):
    tokens, cotangent, route_ids, route_weights, sg, su, sd, eg, eu, ed = args
    ny = lax.axis_size("tensor")
    nq = lax.axis_size("expert") // 2
    nz = min(Z_SIZE, nq)
    t_rows, lanes = tokens.shape
    hid, feats = sg.shape
    half = ny // 2
    eg, eu, ed = (w.reshape(hid, feats) for w in (eg, eu, ed))
    rows = nq * NB
    vmem, dma = pltpu.VMEM, pltpu.SemaphoreType.DMA
    out = jax.ShapeDtypeStruct((t_rows, lanes), BF16)
    in_vmem = pl.BlockSpec(memory_space=pltpu.VMEM)
    in_any = pl.BlockSpec(memory_space=pl.ANY)
    return pl.pallas_call(
        functools.partial(kernel, (nq, nq // nz, nz, ny)),
        out_shape=(out, out),
        in_specs=[in_vmem] * 4 + [in_any] * 6,
        out_specs=(in_vmem, in_vmem),
        scratch_shapes=[
            *[vmem((hid, feats), BF16)] * 6,
            vmem((2, nq, t_rows), F32),
            vmem((2, nq, t_rows), F32),
            vmem((2, t_rows, lanes), BF16),
            vmem((2, ny, t_rows, lanes), BF16),
            vmem((nq, 2 * NB, lanes), BF16),
            vmem((nq, 2 * NB, lanes), BF16),
            vmem((2, 2, ny, rows // 2, lanes), BF16),
            vmem((2, 2, 2, half, rows // 2, lanes), BF16),
            vmem((2, 2, 2, half, rows // 2, lanes), BF16),
            vmem((2, 2, half, t_rows, lanes), BF16),
            vmem((2, 2, half, t_rows, lanes), BF16),
            vmem((nq, 2 * NB, lanes), BF16),
            vmem((nq, 2 * NB, lanes), BF16),
            *[vmem((nq, NA, n * lanes), BF16) for n in (NEAR, ny - NEAR)] * 4,
            vmem((2, t_rows, lanes), F32),
            vmem((2, t_rows, lanes), F32),
            vmem((3, t_rows, hid), F32),
            vmem((2, 3, rows // 2, hid), F32),
            vmem((3, nq * NA, hid), F32),
            vmem((2, 3, t_rows, rows), BF16),
            vmem((3, t_rows, nq * NA), BF16),
            dma((6,)),
            dma((4,)),
            dma((4,)),
            dma((3,)),
            dma((3, 2, 2, half)),
            dma((3,)),
            dma((3, 2, 2, half)),
            dma((8,)),
            dma((8,)),
            pltpu.SemaphoreType.REGULAR,
        ],
        compiler_params=pltpu.CompilerParams(
            collective_id=0, has_side_effects=True, vmem_limit_bytes=56 * 2**20
        ),
        name="routed_layer",
    )(tokens, cotangent, route_ids.T, route_weights.T, sg, su, sd, eg, eu, ed)


def solution(mesh):
    in_specs = (
        P("expert", "tensor"),
        P("expert", "tensor"),
        P("expert", None),
        P("expert", None),
        P("tensor", None),
        P("tensor", None),
        P("tensor", None),
        P("expert", "tensor", None),
        P("expert", "tensor", None),
        P("expert", "tensor", None),
    )
    out_specs = (P("expert", "tensor"), P("expert", "tensor"))
    return jax.shard_map(
        on_device, mesh=mesh, in_specs=in_specs, out_specs=out_specs, check_vma=False
    )
```

```python
import functools

import jax
import jax.numpy as jnp
from jax import lax
from jax.experimental import pallas as pl
from jax.experimental.pallas import tpu as pltpu
from jax.sharding import PartitionSpec as P

MESH = pl.DeviceIdType.MESH
F32 = jnp.float32
BF16 = jnp.bfloat16
CAP = 6
Z_SIZE = 8
WIDE = 4
OWN_ROWS = (4, 5)
SIB_ROWS = (0, 1, 2, 3, 4, 5)
NB = len(OWN_ROWS) + len(SIB_ROWS)
NA = 2 * WIDE
NEAR = 3


def nt_dot(a, b):
    return lax.dot_general(a, b, (((1,), (1,)), ((), ())), preferred_element_type=F32)


def nn_dot(a, b):
    return jnp.dot(a, b, preferred_element_type=F32)


def silu_parts(v):
    s = jax.nn.sigmoid(v)
    return v * s, s * (1.0 + v * (1.0 - s))


def slot_ranks(shape, first, ranks):
    i = lax.broadcasted_iota(jnp.int32, shape, 1)
    inside = (i >= first) & (i < first + len(ranks))
    return jnp.where(inside, i - first + ranks[0], -1).astype(F32)


def kernel(
    dims,
    tok,
    cot,
    ids,
    wts,
    sg_h,
    su_h,
    sd_h,
    eg_h,
    eu_h,
    ed_h,
    out,
    sg,
    su,
    sd,
    eg,
    eu,
    ed,
    meta_out,
    meta_in,
    sib,
    full,
    b_send,
    b_recv,
    b_full,
    r_out,
    r_in,
    t_out,
    t_in,
    ret_send,
    ret_recv,
    near_send,
    far_send,
    near_recv,
    far_recv,
    near_back,
    far_back,
    near_home,
    far_home,
    fin_out,
    fin_in,
    acc_s,
    acc_b,
    acc_a,
    comb,
    comb_a,
    w_sem,
    sib_send,
    sib_recv,
    ag_send,
    ag_recv,
    rs_send,
    rs_recv,
    a2a_send,
    a2a_recv,
    round_sem,
):
    nq, nx, nz, ny = dims
    t_rows, lanes = tok.shape
    half = ny // 2
    e_me = lax.axis_index("expert")
    y = lax.axis_index("tensor")
    core = e_me % 2
    q = e_me // 2
    x = q // nz
    z = q % nz
    sibling = (e_me + 1 - 2 * core, y)
    sides = ((e_me, (y + 1) % ny), (e_me, (y + ny - 1) % ny))
    pairs = [(kind, way) for kind in range(2) for way in range(2)]
    offsets = [0]
    for s in range(1, half):
        offsets += [-s, s]
    offsets += [half]

    def block_at(off):
        return lax.rem(y + off + ny, ny)

    def at_offset(d, sign):
        dx = lax.div(d, nz) if not isinstance(d, int) else d // nz
        dz = lax.rem(d, nz) if not isinstance(d, int) else d % nz
        xx = lax.rem(x + dx if sign > 0 else x - dx + nx, nx)
        zz = lax.rem(z + dz if sign > 0 else z - dz + nz, nz)
        return (2 * (xx * nz + zz) + core, y)

    def send(src, dst, s_sem, r_sem, dev):
        return pltpu.make_async_remote_copy(
            src_ref=src, dst_ref=dst, send_sem=s_sem, recv_sem=r_sem, device_id=dev, device_id_type=MESH
        )

    def cols(ref, blk):
        return ref[:, pl.ds(pl.multiple_of(blk * lanes, lanes), lanes)]

    barrier = pltpu.get_barrier_semaphore()
    column = [at_offset(k * nz, 1) for k in range(1, nx)]
    greeted = [*sides, sibling, *column, *(at_offset(k, 1) for k in range(1, nz))]
    for dev in greeted:
        pl.semaphore_signal(barrier, inc=1, device_id=dev, device_id_type=MESH)

    loads = [
        pltpu.make_async_copy(h, v, w_sem.at[k])
        for k, (h, v) in enumerate(
            ((sg_h, sg), (su_h, su), (sd_h, sd), (eg_h, eg), (eu_h, eu), (ed_h, ed))
        )
    ]
    for load in loads:
        load.start()

    full[0, y] = tok[...]
    full[1, y] = cot[...]

    def steps_of(kind, way):
        return half if (kind + way) % 2 == 0 else half - 1

    def ag_copy(buf, group, kind, way, s):
        at = buf.at[kind, block_at(-s if way == 0 else s)]
        return send(at, at, ag_send.at[group], ag_recv.at[group, kind, way, s], sides[way])

    def ag_start(buf, group):
        for kind, way in pairs:
            ag_copy(buf, group, kind, way, 0).start()

    def ag_step(buf, group, s):
        for kind, way in pairs:
            ag_copy(buf, group, kind, way, s - 1).wait_recv()
            if s < steps_of(kind, way):
                ag_copy(buf, group, kind, way, s).start()

    def ag_last(buf, group):
        for kind, way in pairs:
            if steps_of(kind, way) == half:
                ag_copy(buf, group, kind, way, half - 1).wait_recv()

    def all_sent(ref, sem):
        pltpu.make_async_copy(ref, ref, sem).wait()

    pl.semaphore_wait(barrier, len(greeted))
    ag_start(full, 0)
    to_sib = [
        send(tok, sib.at[0], sib_send.at[1], sib_recv.at[1], sibling),
        send(cot, sib.at[1], sib_send.at[2], sib_recv.at[2], sibling),
    ]
    for copy in to_sib:
        copy.start()
    for dev in column:
        pl.semaphore_signal(round_sem, inc=1, device_id=dev, device_id_type=MESH)

    line = lax.broadcasted_iota(jnp.int32, (2 * nq, t_rows), 0)
    d_of = line % nq
    xx = (x + d_of // nz) % nx
    zz = (z + d_of % nz) % nz
    e_of = 2 * (xx * nz + zz) + jnp.where(line < nq, core, 1 - core)
    named = jnp.zeros((2 * nq, t_rows), F32)
    weight = jnp.zeros((2 * nq, t_rows), F32)
    for k in range(ids.shape[0]):
        hit = ids[k : k + 1, :] == e_of
        named = named + jnp.where(hit, 1.0, 0.0)
        weight = weight + jnp.where(hit, wts[k : k + 1, :], 0.0)
    row = lax.broadcasted_iota(jnp.int32, (t_rows, t_rows), 0)
    col = lax.broadcasted_iota(jnp.int32, (t_rows, t_rows), 1)
    before = jnp.where(row < col, 1.0, 0.0).astype(BF16)
    rank = jnp.where(named > 0.0, nn_dot(named.astype(BF16), before), 1000.0)
    meta_out[0] = rank[nq:]
    meta_out[1] = weight[nq:]

    to_sib.append(send(meta_out, meta_in, sib_send.at[0], sib_recv.at[0], sibling))
    to_sib[2].start()

    def first_layer(acc, v, g, weights, blk, first):
        gate, up, down = weights
        for k, (rows, w) in enumerate(((v, gate), (v, up), (g, down))):
            term = nt_dot(rows, cols(w, blk))
            acc[k] = term if first else acc[k] + term

    def shared_first(off):
        blk = block_at(off)
        first_layer(acc_s, full[0, blk], full[1, blk], (sg, su, sd), blk, off == 0)

    def routed_first(h, off):
        blk = block_at(off)
        first_layer(acc_b.at[h], b_full[h, 0, blk], b_full[h, 1, blk], (eg, eu, ed), blk, off == 0)

    shape = (nq, NB, t_rows)
    own_rank = slot_ranks(shape, 0, OWN_ROWS)
    sib_rank = slot_ranks(shape, len(OWN_ROWS), SIB_ROWS)

    def place(rank_rows, weight_rows, wanted):
        n = wanted.shape[1]
        pick = jnp.where(rank_rows.reshape(nq, 1, t_rows) == wanted, 1.0, 0.0)
        scaled = pick * weight_rows.reshape(nq, 1, t_rows)
        return pick.reshape(nq * n, t_rows), scaled.reshape(nq * n, t_rows)

    own_pick, own_scaled = place(rank[:nq], weight[:nq], own_rank)
    ag_step(full, 0, 1)
    for copy in to_sib:
        copy.wait_recv()
    sib_pick, sib_scaled = place(meta_in[0], meta_in[1], sib_rank)
    slot_weight = jnp.sum(own_scaled, axis=1, keepdims=True) + jnp.sum(sib_scaled, axis=1, keepdims=True)
    own_bf, sib_bf = own_pick.astype(BF16), sib_pick.astype(BF16)
    x_rows = nn_dot(own_bf, tok[...]) + nn_dot(sib_bf, sib[0])
    g_rows = slot_weight * (nn_dot(own_bf, cot[...]) + nn_dot(sib_bf, sib[1]))
    slabs = jnp.concatenate((x_rows.reshape(nq, NB, lanes), g_rows.reshape(nq, NB, lanes)), axis=1)
    b_send[...] = slabs.astype(BF16)

    mid = nq // 2
    swaps = []

    class Swap:
        def __init__(self, src, dst, sign, first=1, last=nq):
            self.k = len(swaps)
            self.src, self.dst, self.sign, self.first, self.last = src, dst, sign, first, last
            swaps.append(self)

        def start(self, first=None, last=None):
            @pl.loop(self.first if first is None else first, self.last if last is None else last)
            def _(d):
                dev = at_offset(d, self.sign)
                send(self.src.at[d], self.dst.at[d], a2a_send.at[self.k], a2a_recv.at[self.k], dev).start()

        def part(self, ref):
            return ref.at[pl.ds(self.first, self.last - self.first)]

        def wait(self):
            all_sent(self.part(self.dst), a2a_recv.at[self.k])

        def end(self):
            all_sent(self.part(self.src), a2a_send.at[self.k])

    b_out = [Swap(b_send, b_recv, 1, max(1, h * mid), (h + 1) * mid) for h in range(2)]
    near_out = Swap(near_send, near_recv, 1)
    far_out = Swap(far_send, far_recv, 1)
    far_in = Swap(far_back, far_home, -1)
    near_in = Swap(near_back, near_home, -1)
    b_in = [Swap(ret_send, ret_recv, -1, max(1, h * mid), (h + 1) * mid) for h in range(2)]

    if nx > 1:
        pl.semaphore_wait(round_sem, nx - 1)
    b_out[0].start()
    if half > 2:
        ag_step(full, 0, 2)
    b_out[1].start()
    b_recv[0] = b_send[0]

    slot = lax.broadcasted_iota(jnp.int32, (nq, NA, t_rows), 1)
    wide_rank = jnp.where(slot < WIDE, slot, slot - WIDE).astype(F32)
    wide_pick, wide_scaled = place(rank[:nq], weight[:nq], wide_rank)
    slot = slot.reshape(nq * NA, t_rows)
    top = slot < WIDE
    x_pick = jnp.where(top, wide_pick, 0.0).astype(BF16)
    g_pick = jnp.where(top, 0.0, wide_pick).astype(BF16)
    slot = lax.broadcasted_iota(jnp.int32, (nq, NA, 1), 1).reshape(nq * NA, 1)
    row_scale = jnp.where(slot < WIDE, 1.0, jnp.sum(wide_scaled, axis=1, keepdims=True))

    def wide_rows(p):
        blk = block_at(offsets[p])
        rows = row_scale * (nn_dot(x_pick, full[0, blk]) + nn_dot(g_pick, full[1, blk]))
        rows = rows.reshape(nq, NA, lanes).astype(BF16)
        if p < NEAR:
            near_send[:, :, p * lanes : (p + 1) * lanes] = rows
        else:
            far_send[:, :, (p - NEAR) * lanes : (p - NEAR + 1) * lanes] = rows

    def unpack_slabs(ref, h):
        v = ref[h * mid : (h + 1) * mid].astype(F32)
        return [v[:, k * NB : (k + 1) * NB].reshape(mid * NB, lanes) for k in range(2)]

    for p in range(NEAR):
        wide_rows(p)
    near_out.start(1, mid)
    for s in range(3, half):
        ag_step(full, 0, s)
    near_out.start(mid, nq)
    for h in range(2):
        b_out[h].wait()
        for kind, v in enumerate(unpack_slabs(b_recv, h)):
            b_full[h, kind, y] = v.astype(BF16)
        ag_start(b_full.at[h], 1 + h)
    near_recv[0] = near_send[0]
    ag_last(full, 0)
    for p in range(NEAR, ny):
        wide_rows(p)
    far_recv[0] = far_send[0]
    far_out.start(1, mid)

    def middle(gate, up, grad):
        act, slope = silu_parts(gate)
        return (
            (act * up).astype(BF16),
            (grad * up * slope).astype(BF16),
            (grad * act).astype(BF16),
        )

    def second_layer(mid, weights):
        hidden, grad_gate, grad_up = mid
        gate, up, down = weights

        def of(kind, blk):
            if kind == 0:
                return nn_dot(hidden, cols(down, blk))
            return nn_dot(grad_gate, cols(gate, blk)) + nn_dot(grad_up, cols(up, blk))

        return of

    for load in loads:
        load.wait()
    def take_wide(p):
        ref, at = (near_recv, p) if p < NEAR else (far_recv, p - NEAR)
        v = ref[:, :, at * lanes : (at + 1) * lanes].astype(F32).reshape(nq * NA, lanes).astype(BF16)
        first_layer(acc_a, v, v, (eg, eu, ed), block_at(offsets[p]), p == 0)

    todo = list(offsets)
    turns = [(s, h) for s in range(1, half) for h in range(2)]
    for n, (s, h) in enumerate(turns):
        ag_step(b_full.at[h], 1 + h, s)
        if n == 1:
            far_out.start(mid, nq)
        if n == len(turns) - 1:
            near_out.wait()
            for p in range(NEAR):
                take_wide(p)
        for off in ([0] if s == 1 else []) + [-s, s]:
            routed_first(h, off)
        share = -(-len(todo) // (len(turns) - n))
        for off in todo[:share]:
            shared_first(off)
        todo = todo[share:]
    shared_mid = middle(acc_s[0], acc_s[1], acc_s[2])

    def rs_offset(kind, way, s):
        far = steps_of(kind, way) - s
        return far if way == 0 else -far

    def rs_copy(o, i, group, kind, way, s):
        return send(
            o.at[kind, way, s],
            i.at[kind, way, s],
            rs_send.at[group],
            rs_recv.at[group, kind, way, s],
            sides[way],
        )

    def rs_step(o, i, group, s, compute):
        for kind, way in pairs:
            if s < steps_of(kind, way):
                term = compute(kind, rs_offset(kind, way, s))
                if s > 0:
                    rs_copy(o, i, group, kind, way, s - 1).wait_recv()
                    term = term + i[kind, way, s - 1].astype(F32)
                o[kind, way, s] = term.astype(BF16)
                rs_copy(o, i, group, kind, way, s).start()

    def rs_total(o, i, group, compute):
        totals = [compute(kind, 0) for kind in range(2)]
        for kind, way in pairs:
            n = steps_of(kind, way)
            rs_copy(o, i, group, kind, way, n - 1).wait_recv()
            totals[kind] = totals[kind] + i[kind, way, n - 1].astype(F32)
        return totals

    second_b = []

    def routed_term(h):
        return lambda kind, off: second_b[h](kind, block_at(off))

    def routed_step(h, s):
        rs_step(r_out.at[h], r_in.at[h], 1 + h, s, routed_term(h))

    for h in range(2):
        ag_last(b_full.at[h], 1 + h)
        routed_first(h, half)
        second_b.append(second_layer(middle(acc_b[h, 0], acc_b[h, 1], acc_b[h, 2]), (eg, eu, ed)))
        routed_step(h, 0)

    far_out.wait()
    for p in range(NEAR, ny):
        take_wide(p)
    hid = sg.shape[0]
    slot = lax.broadcasted_iota(jnp.int32, (nq, NA, hid), 1).reshape(nq * NA, hid)
    top_hid = slot < WIDE
    gate_a, up_a = acc_a[0], acc_a[1]
    act, slope = silu_parts(gate_a)
    hidden_a = jnp.where(top_hid, act * up_a, 0.0).astype(BF16)

    def lowered(v):
        v = v.reshape(nq, NA, hid)
        return jnp.concatenate((v[:, WIDE:], v[:, :WIDE]), axis=1).reshape(nq * NA, hid)

    grad_a = acc_a[2]
    grad_gate_a = jnp.where(top_hid, 0.0, grad_a * lowered(up_a) * lowered(slope)).astype(BF16)
    grad_up_a = jnp.where(top_hid, 0.0, grad_a * lowered(act)).astype(BF16)
    wide_second = second_layer((hidden_a, grad_gate_a, grad_up_a), (eg, eu, ed))

    def wide_back(p):
        blk = block_at(offsets[p])
        rows = (wide_second(0, blk) + wide_second(1, blk)).reshape(nq, NA, lanes).astype(BF16)
        if p < NEAR:
            near_back[:, :, p * lanes : (p + 1) * lanes] = rows
        else:
            far_back[:, :, (p - NEAR) * lanes : (p - NEAR + 1) * lanes] = rows

    for p in range(NEAR, ny):
        wide_back(p)
    far_in.start(1, mid)
    routed_step(0, 1)
    far_in.start(mid, nq)
    far_home[0] = far_back[0]
    routed_step(1, 1)
    for p in range(NEAR):
        wide_back(p)
    near_home[0] = near_back[0]
    for s in range(2, half):
        for h in range(2):
            routed_step(h, s)
            if s == 2:
                near_in.start(max(1, h * mid), (h + 1) * mid)
    if half < 3:
        near_in.start()

    for k, (pick, scaled) in enumerate(((own_pick, own_scaled), (sib_pick, sib_scaled))):
        high = scaled.astype(BF16).astype(F32)
        comb[k, 0] = pick.T.astype(BF16)
        comb[k, 1] = high.T.astype(BF16)
        comb[k, 2] = (scaled - high).T.astype(BF16)
    wide_scaled = jnp.where(top, wide_scaled, 0.0)
    high = wide_scaled.astype(BF16).astype(F32)
    comb_a[0] = jnp.where(top, 0.0, wide_pick).T.astype(BF16)
    comb_a[1] = high.T.astype(BF16)
    comb_a[2] = (wide_scaled - high).T.astype(BF16)

    shared_second = second_layer(shared_mid, (sg, su, sd))

    def token_term(kind, off):
        p = offsets.index(off if -off != half else half)
        home, at = (near_home, p) if p < NEAR else (far_home, p - NEAR)
        rows = home[:, :, at * lanes : (at + 1) * lanes]
        rows = rows.astype(F32).reshape(nq * NA, lanes).astype(BF16)
        total = shared_second(kind, block_at(off))
        if kind == 0:
            return total + nn_dot(comb_a[1], rows) + nn_dot(comb_a[2], rows)
        return total + nn_dot(comb_a[0], rows)

    def send_home(h):
        pair = rs_total(r_out.at[h], r_in.at[h], 1 + h, routed_term(h))
        slabs = jnp.concatenate([v.reshape(mid, NB, lanes) for v in pair], axis=1)
        ret_send[h * mid : (h + 1) * mid] = slabs.astype(BF16)
        b_in[h].start()

    send_home(0)
    near_from = half - 2
    far_in.wait()
    for s in range(half):
        if s == near_from:
            near_in.wait()
        rs_step(t_out, t_in, 0, s, token_term)
        if s == 0:
            send_home(1)
            ret_recv[0] = ret_send[0]

    for swap in b_in:
        swap.wait()
    halves = [unpack_slabs(ret_recv, h) for h in range(2)]
    value_r, input_r = (jnp.concatenate([v[k] for v in halves], axis=0).astype(BF16) for k in range(2))

    fin_out[0] = nn_dot(comb[1, 1], value_r) + nn_dot(comb[1, 2], value_r)
    fin_out[1] = nn_dot(comb[1, 0], input_r)
    last = send(fin_out, fin_in, sib_send.at[3], sib_recv.at[3], sibling)
    last.start()
    value_t, input_t = rs_total(t_out, t_in, 0, token_term)
    value_t = value_t + nn_dot(comb[0, 1], value_r) + nn_dot(comb[0, 2], value_r)
    input_t = input_t + nn_dot(comb[0, 0], input_r)
    last.wait_recv()
    out[0] = (value_t + fin_in[0]).astype(out.dtype)
    out[1] = (input_t + fin_in[1]).astype(out.dtype)

    for group, buf in enumerate((full, b_full.at[0], b_full.at[1])):
        sent = buf.at[:, pl.ds(0, ny - 1)]
        all_sent(sent, ag_send.at[group])
        all_sent(sent, rs_send.at[group])
    for copy in (*to_sib, last):
        copy.wait_send()
    for swap in swaps:
        swap.end()


def on_device(*args):
    tokens, cotangent, route_ids, route_weights, sg, su, sd, eg, eu, ed = args
    ny = lax.axis_size("tensor")
    nq = lax.axis_size("expert") // 2
    nz = min(Z_SIZE, nq)
    t_rows, lanes = tokens.shape
    hid, feats = sg.shape
    half = ny // 2
    eg, eu, ed = (w.reshape(hid, feats) for w in (eg, eu, ed))
    rows = nq * NB
    vmem, dma = pltpu.VMEM, pltpu.SemaphoreType.DMA
    in_vmem = pl.BlockSpec(memory_space=pltpu.VMEM)
    in_any = pl.BlockSpec(memory_space=pl.ANY)
    both = pl.pallas_call(
        functools.partial(kernel, (nq, nq // nz, nz, ny)),
        out_shape=jax.ShapeDtypeStruct((2, t_rows, lanes), BF16),
        in_specs=[in_vmem] * 4 + [in_any] * 6,
        out_specs=in_vmem,
        scratch_shapes=[
            *[vmem((hid, feats), BF16)] * 6,
            vmem((2, nq, t_rows), F32),
            vmem((2, nq, t_rows), F32),
            vmem((2, t_rows, lanes), BF16),
            vmem((2, ny, t_rows, lanes), BF16),
            vmem((nq, 2 * NB, lanes), BF16),
            vmem((nq, 2 * NB, lanes), BF16),
            vmem((2, 2, ny, rows // 2, lanes), BF16),
            vmem((2, 2, 2, half, rows // 2, lanes), BF16),
            vmem((2, 2, 2, half, rows // 2, lanes), BF16),
            vmem((2, 2, half, t_rows, lanes), BF16),
            vmem((2, 2, half, t_rows, lanes), BF16),
            vmem((nq, 2 * NB, lanes), BF16),
            vmem((nq, 2 * NB, lanes), BF16),
            *[vmem((nq, NA, n * lanes), BF16) for n in (NEAR, ny - NEAR)] * 4,
            vmem((2, t_rows, lanes), F32),
            vmem((2, t_rows, lanes), F32),
            vmem((3, t_rows, hid), F32),
            vmem((2, 3, rows // 2, hid), F32),
            vmem((3, nq * NA, hid), F32),
            vmem((2, 3, t_rows, rows), BF16),
            vmem((3, t_rows, nq * NA), BF16),
            dma((6,)),
            dma((4,)),
            dma((4,)),
            dma((3,)),
            dma((3, 2, 2, half)),
            dma((3,)),
            dma((3, 2, 2, half)),
            dma((8,)),
            dma((8,)),
            pltpu.SemaphoreType.REGULAR,
        ],
        compiler_params=pltpu.CompilerParams(
            collective_id=0, has_side_effects=True, vmem_limit_bytes=56 * 2**20
        ),
        name="routed_layer",
    )(tokens, cotangent, route_ids.T, route_weights.T, sg, su, sd, eg, eu, ed)
    return both[0], both[1]


def solution(mesh):
    in_specs = (
        P("expert", "tensor"),
        P("expert", "tensor"),
        P("expert", None),
        P("expert", None),
        P("tensor", None),
        P("tensor", None),
        P("tensor", None),
        P("expert", "tensor", None),
        P("expert", "tensor", None),
        P("expert", "tensor", None),
    )
    out_specs = (P("expert", "tensor"), P("expert", "tensor"))
    return jax.shard_map(
        on_device, mesh=mesh, in_specs=in_specs, out_specs=out_specs, check_vma=False
    )
```
